32 devices in a mesh: dp: 8 (over z, core), tensor: 4 (over y, x).
Axes of the slice: x: 2, y: 2, z: 4, core: 2. Of those that a mesh axis runs over, the one named last changes fastest.
Arguments:
- features: bfloat16 [2560, 2048], P(('dp', 'tensor')), may hold values from -6 to 6
- w_hidden: bfloat16 [2048, 2048], P(None, 'tensor'), may hold values from -0.125 to 0.125
- w_embed: bfloat16 [2048, 768], P('tensor'), may hold values from -0.125 to 0.125
- members: bfloat16 [8, 512, 768], P('dp', 'tensor'), may hold values from -6 to 6
- doc_owner: int32 [2560, 1], P('dp'), may hold values from 0 to 7; in each aligned block of 80 rows (0 to 79, 80 to 159, ...) at most 20 rows name the same one
- doc_local: int32 [2560], P('dp'), may hold values from 0 to 15
- member_cluster: int32 [8, 512], P('dp', 'tensor'), may hold values from 0 to 15, never falling along the last dimension, each value on 1 to 48 neighbouring positions
- member_valid: int32 [8, 512], P('dp', 'tensor'), may hold values 0 or 1
Outputs:
- best: float32 [2560], P(('dp', 'tensor'))
The draws below stay inside these ranges and needn't reach their ends.
Inputs may be any that keep to these rules, and one draw needn't show every extreme that they name: Among the 80 documents of one device (aligned blocks of doc_owner's rows, in the order of dp then tensor) no owner is named more than 20 times; some owner is named exactly 20 times. `member_cluster`: along each owner's row the clusters never fall; every cluster has 1 to 48 slots.
All inputs are finite; a program needn't handle non-finite values. No bound on the sum of `member_valid` on one device may be relied on, other than what follows from the above.
Results may differ from the reference program's by a relative error of at most 0.013.
Values may be sent and summed in bfloat16 or wider, within the bound.
A program may use at most 64 MiB of HBM per device.

```python
import math
import jax
import jax.numpy as jnp
import numpy as np
from jax import lax

HID = 2048
EMB = 768
DOC_TP = 80
CL_DEV = 16
CAP = 20
DOCS = 2560
MEM_OWN = 512
N_DP = 8
N_TENSOR = 4


def place_ends(array, own_key, least, largest):
    longest = array.shape.index(max(array.shape))
    spots = []
    for shift in (0, 1):
        where = [jax.random.randint(jax.random.fold_in(own_key, axis), (), 0, length) for axis, length in enumerate(array.shape)]
        where[longest] = (where[longest] + shift) % array.shape[longest]
        spots.append(tuple(where))
    return array.at[spots[0]].set(least).at[spots[1]].set(largest)


def shard_levels(stream_key, extent, pieces, smallest, top_value):
    def one(dim, parts):
        draws = jax.random.uniform(jax.random.fold_in(jax.random.fold_in(stream_key, 6), dim), (parts,), jnp.float32, smallest / len(pieces), top_value / len(pieces))
        return jnp.repeat(jnp.exp(draws), extent[dim] // parts).reshape((-1,) + (1,) * (len(extent) - dim - 1))

    level = one(*pieces[0])
    for cut in pieces[1:]:
        level = level * one(*cut)
    return level


def length_profile(number_of, total, limit, lean):
    loads = [(1 << 20) // math.isqrt(grade ** lean) + 1 for grade in range(2, number_of + 1)]
    surplus, counts = total - limit - (number_of - 1), [1] * (number_of - 1)
    while surplus > 0:
        movable = [i for i in range(number_of - 1) if counts[i] < limit]
        pool, remaining = sum([loads[i] for i in movable]), surplus
        for i in movable:
            extra = min(limit - counts[i], max(1, remaining * loads[i] // pool), surplus)
            counts[i] = counts[i] + extra
            surplus = surplus - extra
    return np.array([limit] + counts)


def ragged_sizes(key, count, total, reach, skew):
    if count == 2:
        one = jax.random.randint(key, (), max(1, total - reach), min(reach, total - 1) + 1)
        return jnp.stack([one, total - one])
    sizes = jnp.asarray(length_profile(count, total, reach, skew), jnp.int32)
    pairs = (count - 1) // 2
    giver, sink = sizes[1:1 + 2 * pairs:2], sizes[2:2 + 2 * pairs:2]
    room = jnp.minimum(giver - 1, reach - sink)
    passed = jax.random.randint(jax.random.fold_in(key, 1), (pairs,), 0, 1 << 20) % (room + 1)
    sizes = sizes.at[1:1 + 2 * pairs:2].set(giver - passed).at[2:2 + 2 * pairs:2].set(sink + passed)
    return sizes[jax.random.permutation(jax.random.fold_in(key, 2), count)]


def routed_block(key, own, number, rows, amount, top, most, skew):
    sequence = jax.random.permutation(key, amount)
    crowded, usual = load_shares(amount, rows * top, most, skew, True), load_shares(amount, rows * top, most, skew, False)
    places = jnp.arange(amount)

    def named(lengths, rotation):
        used = int((lengths > 0).sum())
        fixed = max(1, used // 4)
        passed = fixed + (places - fixed + rotation * (used - fixed)) % max(1, amount - fixed)
        return jnp.zeros((amount,), jnp.int32).at[sequence[jnp.where(places < fixed, places, passed)]].set(jnp.asarray(lengths, jnp.int32))

    lengths = jnp.where(number % 4 == 0, named(crowded, number // 4), named(usual, number - number // 4 - 1))
    mixed = jax.random.permutation(jax.random.fold_in(own, 3), amount)
    source_of, receiver = mixed[0:amount // 2 * 2:2], mixed[1:amount // 2 * 2:2]
    room = jnp.minimum(lengths[source_of] - 1, most - lengths[receiver]) // 2
    room = jnp.where((source_of == sequence[0]) | (receiver == sequence[0]) | (lengths[receiver] == 0), 0, jnp.maximum(room, 0))
    passed = jax.random.randint(jax.random.fold_in(own, 4), (amount // 2,), 0, 1 << 20) % (room + 1)
    lengths = lengths.at[source_of].add(-passed).at[receiver].add(passed)
    labels = jnp.searchsorted(jnp.cumsum(lengths), jnp.arange(rows * top), side="right").astype(jnp.int32)
    table = labels.reshape(top, rows).T
    table = table[jax.random.permutation(jax.random.fold_in(own, 1), rows)]
    rotation = jax.random.randint(jax.random.fold_in(own, 2), (rows, 1), 0, top)
    return jnp.take_along_axis(table, (jnp.arange(top)[None, :] + rotation) % top, axis=1)


def load_shares(count, total, reach, lean, full):
    weights = [(1 << 20) // math.isqrt(standing ** lean) + 1 for standing in range(1, count + 1)]
    largest = reach if full else min(reach, max(-(-total // count), total * weights[0] // sum(weights)))
    least = 1 if total - largest >= count - 1 else 0
    counts, rest = [largest] + [least] * (count - 1), total - largest - least * (count - 1)
    while rest > 0:
        free = [i for i in range(1, count) if counts[i] < largest] or [i for i in range(1, count) if counts[i] < reach]
        mass, budget = sum([weights[i] for i in free]), rest
        for i in free:
            addition = min(reach - counts[i], max(1, budget * weights[i] // mass), rest)
            counts[i] = counts[i] + addition
            rest = rest - addition
    return np.array(counts)


def bell_draw(key, extent, scale, most, pieces=(), kind=jnp.bfloat16):
    array = scale * jax.random.normal(key, extent, jnp.float32)
    if pieces:
        array = array * shard_levels(key, extent, pieces, -0.22, 0.18)
    return jnp.clip(array, -most, most).astype(kind)


def setup_inputs(seed: int = 0) -> dict:
    seeds = jax.random.split(jax.random.key(seed), 9)
    features = bell_draw(seeds[0], (DOCS, HID), 1.0, 6.0, ((0, 32),))
    w_hidden = bell_draw(seeds[1], (HID, HID), HID ** -0.5, 0.125, ((1, 4),))
    w_embed = bell_draw(seeds[2], (HID, EMB), HID ** -0.5, 0.125, ((0, 4),))
    members = bell_draw(seeds[3], (N_DP, MEM_OWN, EMB), 1.0, 6.0, ((0, 8), (1, 4)))
    doc_owner_keys = jax.random.split(jax.random.fold_in(seeds[4], 1), DOCS // DOC_TP)
    doc_owner_turns = jax.random.permutation(jax.random.fold_in(seeds[4], 3), DOCS // DOC_TP)
    doc_owner = jax.vmap(lambda own, number: routed_block(jax.random.fold_in(seeds[4], 2), own, number, DOC_TP, N_DP, 1, CAP, 2))(doc_owner_keys, doc_owner_turns).reshape((DOCS, 1))
    doc_local = place_ends(jax.random.randint(seeds[5], (DOCS,), 0, CL_DEV), jax.random.fold_in(seeds[5], 1), 0, CL_DEV - 1).astype(jnp.int32)
    member_cluster = jax.vmap(lambda own: jnp.searchsorted(jnp.cumsum(ragged_sizes(own, CL_DEV, MEM_OWN, 3 * MEM_OWN // (2 * CL_DEV), 1)), jnp.arange(MEM_OWN), side="right"))(jax.random.split(seeds[6], N_DP)).reshape((N_DP, MEM_OWN)).astype(jnp.int32)
    member_valid = place_ends((jax.random.randint(seeds[7], (N_DP, MEM_OWN), 0, 4) < 3).astype(jnp.int32), jax.random.fold_in(seeds[7], 1), 0, 1)
    return dict(features=features, w_hidden=w_hidden, w_embed=w_embed, members=members, doc_owner=doc_owner, doc_local=doc_local, member_cluster=member_cluster, member_valid=member_valid)


epsilon = 1e-06

def unit_rows(vectors):
    values = vectors.astype(jnp.float32)
    return (values / jnp.sqrt(lax.optimization_barrier(jnp.sum(values * values, axis=-1, keepdims=True)) + epsilon)).astype(jnp.bfloat16)

def reference(features, w_hidden, w_embed, members, doc_owner, doc_local, member_cluster, member_valid):
    hidden = jax.nn.gelu(jnp.dot(features, w_hidden, preferred_element_type=jnp.float32)).astype(jnp.bfloat16)
    block_width = HID // N_TENSOR
    proj = jnp.zeros((DOCS, EMB), jnp.float32)
    for shard in range(N_TENSOR):
        part_rows = hidden[:, shard * block_width:(shard + 1) * block_width]
        part_weight = w_embed[shard * block_width:(shard + 1) * block_width, :]
        term = jnp.dot(part_rows, part_weight, preferred_element_type=jnp.float32).astype(jnp.bfloat16)
        proj = proj + term.astype(jnp.float32)
    query = unit_rows(proj)
    unit = unit_rows(members)
    owner = doc_owner[:, 0]
    onehot = (owner[:, None] == jnp.arange(N_DP, dtype=jnp.int32)[None, :]).astype(jnp.int32)
    ranking = lax.optimization_barrier(jnp.sum((jnp.cumsum(onehot, axis=0) - 1) * onehot, axis=1)).astype(jnp.int32)
    slot_width = N_DP * N_TENSOR * CAP
    table = jnp.full((N_DP, slot_width), DOCS, jnp.int32)
    table = table.at[owner, ranking].set(jnp.arange(DOCS, dtype=jnp.int32))

    def per_owner(owner_index):
        picks = table[owner_index]
        rows_here = jnp.take(query, picks, axis=0, mode='fill', fill_value=0)
        local_here = jnp.take(doc_local, picks, axis=0, mode='fill', fill_value=-1)
        scores = jnp.dot(rows_here.astype(jnp.float32), unit[owner_index].astype(jnp.float32).T)
        allowed = (member_valid[owner_index][None, :] == 1) & (member_cluster[owner_index][None, :] == local_here[:, None])
        return lax.optimization_barrier(jnp.max(jnp.where(allowed, scores, -1.0), axis=1))
    values = lax.map(per_owner, jnp.arange(N_DP, dtype=jnp.int32))
    best = jnp.full((DOCS,), -1.0, jnp.float32)
    return best.at[table.reshape(-1)].set(values.reshape(-1), mode='drop')
```

```python
import functools
import math

import jax
import jax.numpy as jnp
from jax import lax
from jax.experimental import pallas as pl
from jax.experimental.pallas import tpu as pltpu
from jax.sharding import PartitionSpec as P

EPSILON = 1e-06
MESH = pl.DeviceIdType.MESH
F32 = jnp.float32
BF16 = jnp.bfloat16
LOWEST = -1e30
CHUNKS = 2


def iota(shape, dim):
    return lax.broadcasted_iota(jnp.int32, shape, dim).astype(F32)


def to_column(row, size):
    eye = iota((size, size), 0) == iota((size, size), 1)
    return jnp.sum(jnp.where(eye, row, 0.0), axis=1, keepdims=True)


def to_row(column, size):
    eye = iota((size, size), 0) == iota((size, size), 1)
    return jnp.sum(jnp.where(eye, column, 0.0), axis=0, keepdims=True)


class Sizes:
    def __init__(self, n_dp, n_tensor, rows, hid, width, emb, members):
        self.n_dp, self.n_tensor = n_dp, n_tensor
        self.rows, self.hid, self.width, self.emb, self.members = rows, hid, width, emb, members
        self.nx = max(d for d in range(1, math.isqrt(n_tensor) + 1) if n_tensor % d == 0)
        self.ny = n_tensor // self.nx
        self.cap = min(rows, max(2, 2 * rows // n_dp))
        self.whole = self.cap // 16 * 16
        self.rest = self.cap - self.whole
        self.cols = emb // CHUNKS
        self.tiles = self.cols // 128
        self.folded = -(-self.rest * self.tiles // 16) * 16
        self.block = self.whole * self.tiles + self.folded
        self.slots = n_dp * self.cap
        self.lanes = -(-self.slots // 128) * 128


def kernel(
    z,
    features,
    w_hidden,
    w_embed,
    members,
    doc_owner,
    doc_local,
    member_cluster,
    member_valid,
    best,
    feat,
    w1,
    w2,
    raw,
    unit,
    member_tag,
    sums_out,
    sums_in,
    docs_out,
    docs_in,
    tags_out,
    tags_in,
    answer_out,
    answer_in,
    local_sem,
    feat_send,
    feat_recv,
    unit_send,
    unit_recv,
    mtag_send,
    mtag_recv,
    sums_send,
    sums_recv,
    docs_send,
    docs_recv,
    tags_send,
    tags_recv,
    answer_send,
    answer_recv,
):
    p = lax.axis_index("dp")
    t = lax.axis_index("tensor")
    tx, ty = lax.rem(t, z.nx), lax.div(t, z.nx)
    half = z.hid // 2
    sent = []

    def forward_of(j):
        dx, dy = j % z.nx, j // z.nx
        return lax.rem(ty + dy, z.ny) * z.nx + lax.rem(tx + dx, z.nx)

    def source_of(j):
        dx, dy = j % z.nx, j // z.nx
        return lax.rem(ty + z.ny - dy, z.ny) * z.nx + lax.rem(tx + z.nx - dx, z.nx)

    def remote(src, dst, send, recv, **device):
        copy = pltpu.make_async_remote_copy(
            src_ref=src, dst_ref=dst, send_sem=send, recv_sem=recv, device_id=device,
            device_id_type=MESH,
        )
        copy.start()
        sent.append(copy)
        return copy

    barrier = pltpu.get_barrier_semaphore()
    for j in range(1, z.n_tensor):
        pl.semaphore_signal(barrier, inc=1, device_id={"tensor": forward_of(j)}, device_id_type=MESH)
    for k in range(1, z.n_dp):
        pl.semaphore_signal(
            barrier, inc=1, device_id={"dp": lax.rem(p + k, z.n_dp)}, device_id_type=MESH
        )

    own = [
        pltpu.make_async_copy(features.at[:, pl.ds(h * half, half)], feat.at[h, 0], local_sem.at[h])
        for h in (0, 1)
    ]
    load_w1 = [
        pltpu.make_async_copy(
            w_hidden.at[pl.ds(h * half, half)], w1.at[pl.ds(h * half, half)], local_sem.at[2 + h]
        )
        for h in (0, 1)
    ]
    load_w2 = pltpu.make_async_copy(w_embed, w2, local_sem.at[4])
    load_members = pltpu.make_async_copy(members.at[0], raw, local_sem.at[5])
    for copy in (*own, *load_w1, load_w2, load_members):
        copy.start()

    pl.semaphore_wait(barrier, z.n_tensor - 1 + z.n_dp - 1)

    feat_copy = {}

    def send_feature(h, j, src, target):
        feat_copy[h, j] = remote(
            src, feat.at[h, j], feat_send.at[h, j], feat_recv.at[h, j], tensor=forward_of(target)
        )

    along_x = [dx for dx in range(1, z.nx)]
    along_y = [dy * z.nx for dy in range(1, z.ny)]
    for first in (0, 1):
        for j in along_x:
            h = first
            send_feature(h, j, features.at[:, pl.ds(h * half, half)], j)
        for j in along_y:
            h = 1 - first
            send_feature(h, j, features.at[:, pl.ds(h * half, half)], j)

    rows, wide = z.rows, doc_owner.shape[1]
    mine = iota((rows, wide), 1) == iota((rows, wide), 0) + (t * rows).astype(F32)
    owner = jnp.sum(jnp.where(mine, doc_owner[...].astype(F32), 0.0), axis=1, keepdims=True)
    local = jnp.sum(jnp.where(mine, doc_local[...].astype(F32), 0.0), axis=1, keepdims=True)
    step = owner - p.astype(F32)
    step = jnp.where(step < 0.0, step + float(z.n_dp), step)
    step_row = to_row(step, rows)
    same = step == step_row
    above = iota((rows, rows), 0)
    across = iota((rows, rows), 1)
    rank = jnp.sum(jnp.where(same & (across < above), 1.0, 0.0), axis=1, keepdims=True)
    rank_row = jnp.sum(jnp.where(same & (above < across), 1.0, 0.0), axis=0, keepdims=True)
    place = jnp.where(
        rank < float(z.whole),
        step * float(z.whole) + rank,
        float(z.n_dp * z.whole) + step * float(z.rest) + rank - float(z.whole),
    )
    placed = iota((rows, z.lanes), 1) == place
    step_hot = jnp.where(iota((z.n_dp, rows), 0) == step_row, 1.0, 0.0).astype(BF16)
    tags = jnp.dot(
        step_hot,
        jnp.where(placed, local + 1.0, 0.0).astype(BF16),
        preferred_element_type=F32,
    )
    for k in range(z.n_dp):
        tags_out[k] = tags[k : k + 1, :]
    tags_copy = [
        remote(
            tags_out.at[k], tags_in.at[k], tags_send.at[k], tags_recv.at[k],
            dp=lax.rem(p + k, z.n_dp),
        )
        for k in range(1, z.n_dp)
    ]

    member_tag[0] = jnp.where(
        member_valid[...] == 1, member_cluster[...].astype(F32) + 1.0, -1.0
    )
    load_members.wait()
    values = raw[...].astype(F32)
    unit[0] = (
        values / jnp.sqrt(jnp.sum(values * values, axis=1, keepdims=True) + EPSILON)
    ).astype(BF16)

    def head(j):
        total = jnp.dot(feat[0, j], w1[:half, :], preferred_element_type=F32)
        total += jnp.dot(feat[1, j], w1[half:, :], preferred_element_type=F32)
        hidden = jax.nn.gelu(total).astype(BF16)
        for c in range(CHUNKS):
            sums_out[c, j] = jnp.dot(
                hidden, w2[:, c * z.cols : (c + 1) * z.cols], preferred_element_type=F32
            ).astype(BF16)
            if j:
                sums_copy[c, j] = remote(
                    sums_out.at[c, j], sums_in.at[c, j], sums_send.at[c, j], sums_recv.at[c, j],
                    tensor=source_of(j),
                )

    sums_copy = {}
    for copy in (*own, *load_w1, load_w2):
        copy.wait()
    head(0)

    for j in along_x:
        feat_copy[0, j].wait_recv()
        for dy in along_y:
            send_feature(0, j + dy, feat.at[0, j], dy)
    for j in along_y:
        feat_copy[1, j].wait_recv()
        for dx in along_x:
            send_feature(1, j + dx, feat.at[1, j], dx)
    for j in along_x:
        feat_copy[1, j].wait_recv()
        head(j)
    for j in along_y:
        feat_copy[0, j].wait_recv()
        head(j)
    for dy in along_y:
        for dx in along_x:
            feat_copy[0, dy + dx].wait_recv()
            feat_copy[1, dy + dx].wait_recv()
            head(dy + dx)

    unit_copy = []
    for j in range(1, z.n_tensor):
        target = forward_of(j)
        unit_copy.append(
            remote(unit.at[0], unit.at[j], unit_send.at[j], unit_recv.at[j], tensor=target)
        )
        unit_copy.append(
            remote(
                member_tag.at[0], member_tag.at[j], mtag_send.at[j], mtag_recv.at[j], tensor=target
            )
        )

    code = step_row * float(z.cap) + rank_row
    code = code.reshape(1, 1, rows)
    if z.whole:
        shape = (z.n_dp, z.whole, rows)
        pack_whole = jnp.where(
            code == iota(shape, 0) * float(z.cap) + iota(shape, 1), 1.0, 0.0
        ).reshape(z.n_dp * z.whole, rows).astype(BF16)
    pack_rest = []
    if z.rest:
        shape = (z.n_dp, z.folded, rows)
        for c in range(z.tiles):
            at = iota(shape, 1) - float(c * z.rest)
            inside = (at >= 0.0) & (at < float(z.rest))
            hit = inside & (code == iota(shape, 0) * float(z.cap) + float(z.whole) + at)
            pack_rest.append(
                jnp.where(hit, 1.0, 0.0).reshape(z.n_dp * z.folded, rows).astype(BF16)
            )

    square = jnp.zeros((rows, 1), F32)
    docs_copy = {}
    for c in range(CHUNKS):
        proj = sums_out[c, 0].astype(F32)
        for j in range(1, z.n_tensor):
            sums_copy[c, j].wait_recv()
            proj += sums_in[c, j].astype(F32)
        query = proj.astype(BF16)
        if z.whole:
            packed = jnp.dot(pack_whole, query, preferred_element_type=F32).astype(BF16)
        if z.rest:
            tail = jnp.zeros((z.n_dp * z.folded, 128), F32)
            for i in range(z.tiles):
                tail += jnp.dot(
                    pack_rest[i], query[:, i * 128 : (i + 1) * 128], preferred_element_type=F32
                )
            tail = tail.astype(BF16)
        for k in [*range(1, z.n_dp), 0]:
            target = docs_out if k else docs_in
            if z.whole:
                for i in range(z.tiles):
                    target[c, k, i * z.whole : (i + 1) * z.whole, :] = packed[
                        k * z.whole : (k + 1) * z.whole, i * 128 : (i + 1) * 128
                    ]
            if z.rest:
                target[c, k, z.tiles * z.whole :, :] = tail[k * z.folded : (k + 1) * z.folded, :]
            if k:
                docs_copy[c, k] = remote(
                    docs_out.at[c, k], docs_in.at[c, k], docs_send.at[c, k], docs_recv.at[c, k],
                    dp=lax.rem(p + k, z.n_dp),
                )
        square += jnp.sum(proj * proj, axis=1, keepdims=True)
    inverse = 1.0 / jnp.sqrt(square + EPSILON)

    tag_row = tags_out[0]
    for k in range(1, z.n_dp):
        tags_copy[k - 1].wait_recv()
        tag_row += tags_in[k]
    tag_row = tag_row[:, : z.slots]
    for copy in unit_copy:
        copy.wait_recv()
    allowed = [to_column(member_tag[j], z.members) for j in range(z.n_tensor)]

    unfold = []
    if z.rest:
        shape = (z.n_dp * z.rest, z.n_dp * z.folded)
        out_row, in_row = iota(shape, 0), iota(shape, 1)
        for i in range(z.tiles):
            hit = jnp.zeros(shape, F32)
            for k in range(z.n_dp):
                at = out_row - float(k * z.rest)
                inside = (at >= 0.0) & (at < float(z.rest))
                hit = jnp.where(
                    inside & (in_row == at + float(k * z.folded + i * z.rest)), 1.0, hit
                )
            unfold.append(hit.astype(BF16))

    scores = [jnp.zeros((z.members, z.slots), F32) for _ in range(z.n_tensor)]
    for c in range(CHUNKS):
        for k in range(1, z.n_dp):
            docs_copy[c, k].wait_recv()
        parts = []
        if z.whole:
            parts.append(
                jnp.concatenate(
                    [
                        docs_in[c, :, i * z.whole : (i + 1) * z.whole, :].reshape(
                            z.n_dp * z.whole, 128
                        )
                        for i in range(z.tiles)
                    ],
                    axis=1,
                )
            )
        if z.rest:
            tail = docs_in[c, :, z.tiles * z.whole :, :].reshape(z.n_dp * z.folded, 128)
            parts.append(
                jnp.concatenate(
                    [
                        jnp.dot(unfold[i], tail, preferred_element_type=F32).astype(BF16)
                        for i in range(z.tiles)
                    ],
                    axis=1,
                )
            )
        arrived = jnp.concatenate(parts, axis=0) if len(parts) > 1 else parts[0]
        for j in range(z.n_tensor):
            scores[j] += lax.dot_general(
                unit[j, :, c * z.cols : (c + 1) * z.cols],
                arrived,
                (((1,), (1,)), ((), ())),
                preferred_element_type=F32,
            )
    top = jnp.full((1, z.slots), LOWEST, F32)
    for j in range(z.n_tensor):
        kept = jnp.where(allowed[j] == tag_row, scores[j], LOWEST)
        top = jnp.maximum(top, jnp.max(kept, axis=0, keepdims=True))
    answer_out[...] = jnp.zeros_like(answer_out)
    answer_out[:, : z.slots] = top

    answer_copy = [
        remote(
            answer_out, answer_in.at[k], answer_send.at[k], answer_recv.at[k],
            dp=lax.rem(p + z.n_dp - k, z.n_dp),
        )
        for k in range(1, z.n_dp)
    ]
    found = jnp.where(step == 0.0, answer_out[...], 0.0)
    for k in range(1, z.n_dp):
        answer_copy[k - 1].wait_recv()
        found = jnp.where(step == float(k), answer_in[k], found)
    value = jnp.sum(jnp.where(placed, found, 0.0), axis=1, keepdims=True)
    best[...] = to_row(jnp.maximum(value * inverse, -1.0), rows)
    for copy in sent:
        copy.wait_send()


def body(features, w_hidden, w_embed, members, doc_owner, doc_local, member_cluster, member_valid):
    n_dp, n_tensor = lax.axis_size("dp"), lax.axis_size("tensor")
    rows, hid = features.shape
    width, emb = w_embed.shape
    z = Sizes(n_dp, n_tensor, rows, hid, width, emb, members.shape[1])
    half = hid // 2
    dma = pltpu.SemaphoreType.DMA
    hbm = pl.BlockSpec(memory_space=pl.ANY)
    vmem = pl.BlockSpec(memory_space=pltpu.VMEM)
    out = pl.pallas_call(
        functools.partial(kernel, z),
        out_shape=jax.ShapeDtypeStruct((1, rows), F32),
        in_specs=[hbm] * 4 + [vmem] * 4,
        out_specs=vmem,
        scratch_shapes=[
            pltpu.VMEM((2, n_tensor, rows, half), BF16),
            pltpu.VMEM((hid, width), BF16),
            pltpu.VMEM((width, emb), BF16),
            pltpu.VMEM((z.members, emb), BF16),
            pltpu.VMEM((n_tensor, z.members, emb), BF16),
            pltpu.VMEM((n_tensor, 1, z.members), F32),
            pltpu.VMEM((CHUNKS, n_tensor, rows, z.cols), BF16),
            pltpu.VMEM((CHUNKS, n_tensor, rows, z.cols), BF16),
            pltpu.VMEM((CHUNKS, n_dp, z.block, 128), BF16),
            pltpu.VMEM((CHUNKS, n_dp, z.block, 128), BF16),
            pltpu.VMEM((n_dp, 1, z.lanes), F32),
            pltpu.VMEM((n_dp, 1, z.lanes), F32),
            pltpu.VMEM((1, z.lanes), F32),
            pltpu.VMEM((n_dp, 1, z.lanes), F32),
            dma((6,)),
            dma((2, n_tensor)),
            dma((2, n_tensor)),
            dma((n_tensor,)),
            dma((n_tensor,)),
            dma((n_tensor,)),
            dma((n_tensor,)),
            dma((CHUNKS, n_tensor)),
            dma((CHUNKS, n_tensor)),
            dma((CHUNKS, n_dp)),
            dma((CHUNKS, n_dp)),
            dma((n_dp,)),
            dma((n_dp,)),
            dma((n_dp,)),
            dma((n_dp,)),
        ],
        compiler_params=pltpu.CompilerParams(
            collective_id=0, has_side_effects=True, vmem_limit_bytes=48 * 1024 * 1024
        ),
        name="match",
    )(
        features,
        w_hidden,
        w_embed,
        members,
        doc_owner.reshape(1, -1),
        doc_local.reshape(1, -1),
        member_cluster,
        member_valid,
    )
    return out.reshape(rows)


def solution(mesh):
    return jax.shard_map(
        body,
        mesh=mesh,
        in_specs=(
            P(("dp", "tensor"), None),
            P(None, "tensor"),
            P("tensor", None),
            P("dp", "tensor", None),
            P("dp", None),
            P("dp"),
            P("dp", "tensor"),
            P("dp", "tensor"),
        ),
        out_specs=P(("dp", "tensor")),
        check_vma=False,
    )
```

```python
import functools
import math

import jax
import jax.numpy as jnp
from jax import lax
from jax.experimental import pallas as pl
from jax.experimental.pallas import tpu as pltpu
from jax.sharding import PartitionSpec as P

EPSILON = 1e-06
MESH = pl.DeviceIdType.MESH
F32 = jnp.float32
BF16 = jnp.bfloat16
LOWEST = -1e30
CHUNKS = 2


def iota(shape, dim):
    return lax.broadcasted_iota(jnp.int32, shape, dim).astype(F32)


def to_column(row, size):
    eye = iota((size, size), 0) == iota((size, size), 1)
    return jnp.sum(jnp.where(eye, row, 0.0), axis=1, keepdims=True)


def to_row(column, size):
    eye = iota((size, size), 0) == iota((size, size), 1)
    return jnp.sum(jnp.where(eye, column, 0.0), axis=0, keepdims=True)


class Sizes:
    def __init__(self, n_dp, n_tensor, rows, hid, width, emb, members):
        self.n_dp, self.n_tensor = n_dp, n_tensor
        self.rows, self.hid, self.width, self.emb, self.members = rows, hid, width, emb, members
        self.nx = max(d for d in range(1, math.isqrt(n_tensor) + 1) if n_tensor % d == 0)
        self.ny = n_tensor // self.nx
        self.cap = min(rows, max(2, 2 * rows // n_dp))
        self.whole = self.cap // 16 * 16
        self.rest = self.cap - self.whole
        self.cols = emb // CHUNKS
        self.tiles = self.cols // 128
        self.folded = -(-self.rest * self.tiles // 16) * 16
        self.block = self.whole * self.tiles + self.folded
        self.slots = n_dp * self.cap
        self.lanes = -(-self.slots // 128) * 128


def kernel(
    z,
    features,
    w_hidden,
    w_embed,
    members,
    hbm_owner,
    hbm_local,
    hbm_cluster,
    hbm_valid,
    best,
    feat,
    w1,
    w2,
    raw,
    doc_owner,
    doc_local,
    member_cluster,
    member_valid,
    unit,
    member_tag,
    sums_out,
    sums_in,
    docs_out,
    docs_in,
    tags_out,
    tags_in,
    answer_out,
    answer_in,
    local_sem,
    feat_send,
    feat_recv,
    unit_send,
    unit_recv,
    mtag_send,
    mtag_recv,
    sums_send,
    sums_recv,
    docs_send,
    docs_recv,
    tags_send,
    tags_recv,
    answer_send,
    answer_recv,
):
    p = lax.axis_index("dp")
    t = lax.axis_index("tensor")
    tx, ty = lax.rem(t, z.nx), lax.div(t, z.nx)
    half = z.hid // 2
    sent = []

    def forward_of(j):
        dx, dy = j % z.nx, j // z.nx
        return lax.rem(ty + dy, z.ny) * z.nx + lax.rem(tx + dx, z.nx)

    def source_of(j):
        dx, dy = j % z.nx, j // z.nx
        return lax.rem(ty + z.ny - dy, z.ny) * z.nx + lax.rem(tx + z.nx - dx, z.nx)

    def remote(src, dst, send, recv, **device):
        copy = pltpu.make_async_remote_copy(
            src_ref=src, dst_ref=dst, send_sem=send, recv_sem=recv, device_id=device,
            device_id_type=MESH,
        )
        copy.start()
        sent.append(copy)
        return copy

    barrier = pltpu.get_barrier_semaphore()
    for j in range(1, z.n_tensor):
        pl.semaphore_signal(barrier, inc=1, device_id={"tensor": forward_of(j)}, device_id_type=MESH)
    for k in range(1, z.n_dp):
        pl.semaphore_signal(
            barrier, inc=1, device_id={"dp": lax.rem(p + k, z.n_dp)}, device_id_type=MESH
        )

    own = [
        pltpu.make_async_copy(features.at[:, pl.ds(h * half, half)], feat.at[h, 0], local_sem.at[h])
        for h in (0, 1)
    ]
    load_w1 = [
        pltpu.make_async_copy(
            w_hidden.at[pl.ds(h * half, half)], w1.at[pl.ds(h * half, half)], local_sem.at[2 + h]
        )
        for h in (0, 1)
    ]
    load_w2 = pltpu.make_async_copy(w_embed, w2, local_sem.at[4])
    load_members = pltpu.make_async_copy(members.at[0], raw, local_sem.at[5])
    load_small = [
        pltpu.make_async_copy(src, dst, local_sem.at[6 + i])
        for i, (src, dst) in enumerate(
            (
                (hbm_owner, doc_owner),
                (hbm_local, doc_local),
                (hbm_cluster, member_cluster),
                (hbm_valid, member_valid),
            )
        )
    ]
    for copy in (*load_small, *own, *load_w1, load_w2, load_members):
        copy.start()

    pl.semaphore_wait(barrier, z.n_tensor - 1 + z.n_dp - 1)

    feat_copy = {}

    def send_feature(h, j, src, target):
        feat_copy[h, j] = remote(
            src, feat.at[h, j], feat_send.at[h, j], feat_recv.at[h, j], tensor=forward_of(target)
        )

    along_x = [dx for dx in range(1, z.nx)]
    along_y = [dy * z.nx for dy in range(1, z.ny)]
    for first in (0, 1):
        for j in along_x:
            h = first
            send_feature(h, j, features.at[:, pl.ds(h * half, half)], j)
        for j in along_y:
            h = 1 - first
            send_feature(h, j, features.at[:, pl.ds(h * half, half)], j)

    for copy in load_small:
        copy.wait()
    rows, wide = z.rows, doc_owner.shape[1]
    mine = iota((rows, wide), 1) == iota((rows, wide), 0) + (t * rows).astype(F32)
    owner = jnp.sum(jnp.where(mine, doc_owner[...].astype(F32), 0.0), axis=1, keepdims=True)
    local = jnp.sum(jnp.where(mine, doc_local[...].reshape(1, wide).astype(F32), 0.0), axis=1, keepdims=True)
    step = owner - p.astype(F32)
    step = jnp.where(step < 0.0, step + float(z.n_dp), step)
    step_row = to_row(step, rows)
    same = step == step_row
    above = iota((rows, rows), 0)
    across = iota((rows, rows), 1)
    rank = jnp.sum(jnp.where(same & (across < above), 1.0, 0.0), axis=1, keepdims=True)
    rank_row = jnp.sum(jnp.where(same & (above < across), 1.0, 0.0), axis=0, keepdims=True)
    place = jnp.where(
        rank < float(z.whole),
        step * float(z.whole) + rank,
        float(z.n_dp * z.whole) + step * float(z.rest) + rank - float(z.whole),
    )
    placed = iota((rows, z.lanes), 1) == place
    step_hot = jnp.where(iota((z.n_dp, rows), 0) == step_row, 1.0, 0.0).astype(BF16)
    tags = jnp.dot(
        step_hot,
        jnp.where(placed, local + 1.0, 0.0).astype(BF16),
        preferred_element_type=F32,
    )
    for k in range(z.n_dp):
        tags_out[k] = tags[k : k + 1, :]
    tags_copy = [
        remote(
            tags_out.at[k], tags_in.at[k], tags_send.at[k], tags_recv.at[k],
            dp=lax.rem(p + k, z.n_dp),
        )
        for k in range(1, z.n_dp)
    ]

    member_tag[0] = jnp.where(
        member_valid[...] == 1, member_cluster[...].astype(F32) + 1.0, -1.0
    )
    load_members.wait()
    values = raw[...].astype(F32)
    unit[:, 0] = (
        (values / jnp.sqrt(jnp.sum(values * values, axis=1, keepdims=True) + EPSILON))
        .astype(BF16)
        .reshape(2, z.members // 2, z.emb)
    )
    mtag_copy = [
        remote(
            member_tag.at[0], member_tag.at[j], mtag_send.at[j], mtag_recv.at[j],
            tensor=forward_of(j),
        )
        for j in range(1, z.n_tensor)
    ]

    def head(j):
        total = jnp.dot(feat[0, j], w1[:half, :], preferred_element_type=F32)
        total += jnp.dot(feat[1, j], w1[half:, :], preferred_element_type=F32)
        hidden = jax.nn.gelu(total).astype(BF16)
        for c in range(CHUNKS):
            sums_out[c, j] = jnp.dot(
                hidden, w2[:, c * z.cols : (c + 1) * z.cols], preferred_element_type=F32
            ).astype(BF16)
            if j:
                sums_copy[c, j] = remote(
                    sums_out.at[c, j], sums_in.at[c, j], sums_send.at[c, j], sums_recv.at[c, j],
                    tensor=source_of(j),
                )

    sums_copy = {}
    for copy in (*own, *load_w1, load_w2):
        copy.wait()
    head(0)

    for j in along_x:
        feat_copy[0, j].wait_recv()
        for dy in along_y:
            send_feature(0, j + dy, feat.at[0, j], dy)
    for j in along_y:
        feat_copy[1, j].wait_recv()
        for dx in along_x:
            send_feature(1, j + dx, feat.at[1, j], dx)
    for j in along_x:
        feat_copy[1, j].wait_recv()
        head(j)
    for j in along_y:
        feat_copy[0, j].wait_recv()
        head(j)
    for dy in along_y:
        for dx in along_x:
            feat_copy[0, dy + dx].wait_recv()
            feat_copy[1, dy + dx].wait_recv()
            head(dy + dx)

    code = step_row * float(z.cap) + rank_row
    code = code.reshape(1, 1, rows)
    if z.whole:
        shape = (z.n_dp, z.whole, rows)
        pack_whole = jnp.where(
            code == iota(shape, 0) * float(z.cap) + iota(shape, 1), 1.0, 0.0
        ).reshape(z.n_dp * z.whole, rows).astype(BF16)
    pack_rest = []
    if z.rest:
        shape = (z.n_dp, z.folded, rows)
        for c in range(z.tiles):
            at = iota(shape, 1) - float(c * z.rest)
            inside = (at >= 0.0) & (at < float(z.rest))
            hit = inside & (code == iota(shape, 0) * float(z.cap) + float(z.whole) + at)
            pack_rest.append(
                jnp.where(hit, 1.0, 0.0).reshape(z.n_dp * z.folded, rows).astype(BF16)
            )

    unit_copy = {}

    def send_unit(h, j, held, target):
        unit_copy[h, j] = remote(
            unit.at[h, held], unit.at[h, j], unit_send.at[h, j], unit_recv.at[h, j],
            tensor=forward_of(target),
        )

    square = jnp.zeros((rows, 1), F32)
    docs_copy = {}
    for c in range(CHUNKS):
        proj = sums_out[c, 0].astype(F32)
        for j in range(1, z.n_tensor):
            sums_copy[c, j].wait_recv()
            proj += sums_in[c, j].astype(F32)
        query = proj.astype(BF16)
        if z.whole:
            packed = jnp.dot(pack_whole, query, preferred_element_type=F32).astype(BF16)
        if z.rest:
            tail = jnp.zeros((z.n_dp * z.folded, 128), F32)
            for i in range(z.tiles):
                tail += jnp.dot(
                    pack_rest[i], query[:, i * 128 : (i + 1) * 128], preferred_element_type=F32
                )
            tail = tail.astype(BF16)
        for k in [*range(1, z.n_dp), 0]:
            target = docs_out if k else docs_in
            if z.whole:
                for i in range(z.tiles):
                    target[c, k, i * z.whole : (i + 1) * z.whole, :] = packed[
                        k * z.whole : (k + 1) * z.whole, i * 128 : (i + 1) * 128
                    ]
            if z.rest:
                target[c, k, z.tiles * z.whole :, :] = tail[k * z.folded : (k + 1) * z.folded, :]
            if k:
                docs_copy[c, k] = remote(
                    docs_out.at[c, k], docs_in.at[c, k], docs_send.at[c, k], docs_recv.at[c, k],
                    dp=lax.rem(p + k, z.n_dp),
                )
        square += jnp.sum(proj * proj, axis=1, keepdims=True)
        if c == 0:
            for first in (0, 1):
                for j in along_x:
                    send_unit(first, j, 0, j)
                for j in along_y:
                    send_unit(1 - first, j, 0, j)
    inverse = 1.0 / jnp.sqrt(square + EPSILON)
    for j in along_x:
        unit_copy[0, j].wait_recv()
        for dy in along_y:
            send_unit(0, j + dy, j, dy)
    for j in along_y:
        unit_copy[1, j].wait_recv()
        for dx in along_x:
            send_unit(1, j + dx, j, dx)

    tag_row = tags_out[0]
    for k in range(1, z.n_dp):
        tags_copy[k - 1].wait_recv()
        tag_row += tags_in[k]
    tag_row = tag_row[:, : z.slots]
    for copy in mtag_copy:
        copy.wait_recv()
    allowed = [to_column(member_tag[j], z.members) for j in range(z.n_tensor)]

    unfold = []
    if z.rest:
        shape = (z.n_dp * z.rest, z.n_dp * z.folded)
        out_row, in_row = iota(shape, 0), iota(shape, 1)
        for i in range(z.tiles):
            hit = jnp.zeros(shape, F32)
            for k in range(z.n_dp):
                at = out_row - float(k * z.rest)
                inside = (at >= 0.0) & (at < float(z.rest))
                hit = jnp.where(
                    inside & (in_row == at + float(k * z.folded + i * z.rest)), 1.0, hit
                )
            unfold.append(hit.astype(BF16))

    arrived = []
    for c in range(CHUNKS):
        for k in range(1, z.n_dp):
            docs_copy[c, k].wait_recv()
        parts = []
        if z.whole:
            parts.append(
                jnp.concatenate(
                    [
                        docs_in[c, :, i * z.whole : (i + 1) * z.whole, :].reshape(
                            z.n_dp * z.whole, 128
                        )
                        for i in range(z.tiles)
                    ],
                    axis=1,
                )
            )
        if z.rest:
            tail = docs_in[c, :, z.tiles * z.whole :, :].reshape(z.n_dp * z.folded, 128)
            parts.append(
                jnp.concatenate(
                    [
                        jnp.dot(unfold[i], tail, preferred_element_type=F32).astype(BF16)
                        for i in range(z.tiles)
                    ],
                    axis=1,
                )
            )
        arrived.append(jnp.concatenate(parts, axis=0) if len(parts) > 1 else parts[0])
    top = jnp.full((1, z.slots), LOWEST, F32)
    for j in range(z.n_tensor):
        if j in along_x:
            unit_copy[1, j].wait_recv()
        elif j in along_y:
            unit_copy[0, j].wait_recv()
        elif j:
            unit_copy[0, j].wait_recv()
            unit_copy[1, j].wait_recv()
        scores = jnp.zeros((z.members, z.slots), F32)
        for c in range(CHUNKS):
            scores += lax.dot_general(
                unit[:, j, :, c * z.cols : (c + 1) * z.cols].reshape(z.members, z.cols),
                arrived[c],
                (((1,), (1,)), ((), ())),
                preferred_element_type=F32,
            )
        kept = jnp.where(allowed[j] == tag_row, scores, LOWEST)
        top = jnp.maximum(top, jnp.max(kept, axis=0, keepdims=True))
    answer_out[...] = jnp.zeros_like(answer_out)
    answer_out[:, : z.slots] = top

    answer_copy = [
        remote(
            answer_out, answer_in.at[k], answer_send.at[k], answer_recv.at[k],
            dp=lax.rem(p + z.n_dp - k, z.n_dp),
        )
        for k in range(1, z.n_dp)
    ]
    found = jnp.where(step == 0.0, answer_out[...], 0.0)
    for k in range(1, z.n_dp):
        answer_copy[k - 1].wait_recv()
        found = jnp.where(step == float(k), answer_in[k], found)
    value = jnp.sum(jnp.where(placed, found, 0.0), axis=1, keepdims=True)
    best[...] = to_row(jnp.maximum(value * inverse, -1.0), rows)
    for copy in sent:
        copy.wait_send()


def body(features, w_hidden, w_embed, members, doc_owner, doc_local, member_cluster, member_valid):
    n_dp, n_tensor = lax.axis_size("dp"), lax.axis_size("tensor")
    rows, hid = features.shape
    width, emb = w_embed.shape
    z = Sizes(n_dp, n_tensor, rows, hid, width, emb, members.shape[1])
    half = hid // 2
    dma = pltpu.SemaphoreType.DMA
    hbm = pl.BlockSpec(memory_space=pl.ANY)
    vmem = pl.BlockSpec(memory_space=pltpu.VMEM)
    out = pl.pallas_call(
        functools.partial(kernel, z),
        out_shape=jax.ShapeDtypeStruct((1, rows), F32),
        in_specs=[hbm] * 8,
        out_specs=vmem,
        scratch_shapes=[
            pltpu.VMEM((2, n_tensor, rows, half), BF16),
            pltpu.VMEM((hid, width), BF16),
            pltpu.VMEM((width, emb), BF16),
            pltpu.VMEM((z.members, emb), BF16),
            pltpu.VMEM((1, doc_owner.shape[0]), jnp.int32),
            pltpu.VMEM(doc_local.shape, jnp.int32),
            pltpu.VMEM((1, z.members), jnp.int32),
            pltpu.VMEM((1, z.members), jnp.int32),
            pltpu.VMEM((2, n_tensor, z.members // 2, emb), BF16),
            pltpu.VMEM((n_tensor, 1, z.members), F32),
            pltpu.VMEM((CHUNKS, n_tensor, rows, z.cols), BF16),
            pltpu.VMEM((CHUNKS, n_tensor, rows, z.cols), BF16),
            pltpu.VMEM((CHUNKS, n_dp, z.block, 128), BF16),
            pltpu.VMEM((CHUNKS, n_dp, z.block, 128), BF16),
            pltpu.VMEM((n_dp, 1, z.lanes), F32),
            pltpu.VMEM((n_dp, 1, z.lanes), F32),
            pltpu.VMEM((1, z.lanes), F32),
            pltpu.VMEM((n_dp, 1, z.lanes), F32),
            dma((10,)),
            dma((2, n_tensor)),
            dma((2, n_tensor)),
            dma((2, n_tensor)),
            dma((2, n_tensor)),
            dma((n_tensor,)),
            dma((n_tensor,)),
            dma((CHUNKS, n_tensor)),
            dma((CHUNKS, n_tensor)),
            dma((CHUNKS, n_dp)),
            dma((CHUNKS, n_dp)),
            dma((n_dp,)),
            dma((n_dp,)),
            dma((n_dp,)),
            dma((n_dp,)),
        ],
        compiler_params=pltpu.CompilerParams(
            collective_id=0, has_side_effects=True, vmem_limit_bytes=62 * 1024 * 1024
        ),
        name="match",
    )(
        features,
        w_hidden,
        w_embed,
        members,
        doc_owner.reshape(1, -1),
        doc_local,
        member_cluster,
        member_valid,
    )
    return out.reshape(rows)


def solution(mesh):
    return jax.shard_map(
        body,
        mesh=mesh,
        in_specs=(
            P(("dp", "tensor"), None),
            P(None, "tensor"),
            P("tensor", None),
            P("dp", "tensor", None),
            P("dp", None),
            P("dp"),
            P("dp", "tensor"),
            P("dp", "tensor"),
        ),
        out_specs=P(("dp", "tensor")),
        check_vma=False,
    )
```

```python
import functools
import math

import jax
import jax.numpy as jnp
from jax import lax
from jax.experimental import pallas as pl
from jax.experimental.pallas import tpu as pltpu
from jax.sharding import PartitionSpec as P

EPSILON = 1e-06
MESH = pl.DeviceIdType.MESH
F32 = jnp.float32
BF16 = jnp.bfloat16
LOWEST = -1e30
CHUNKS = 2


def iota(shape, dim):
    return lax.broadcasted_iota(jnp.int32, shape, dim).astype(F32)


def to_column(row, size):
    eye = iota((size, size), 0) == iota((size, size), 1)
    return jnp.sum(jnp.where(eye, row, 0.0), axis=1, keepdims=True)


def to_row(column, size):
    eye = iota((size, size), 0) == iota((size, size), 1)
    return jnp.sum(jnp.where(eye, column, 0.0), axis=0, keepdims=True)


class Sizes:
    def __init__(self, n_dp, n_tensor, rows, hid, width, emb, members):
        self.n_dp, self.n_tensor = n_dp, n_tensor
        self.rows, self.hid, self.width, self.emb, self.members = rows, hid, width, emb, members
        self.nx = max(d for d in range(1, math.isqrt(n_tensor) + 1) if n_tensor % d == 0)
        self.ny = n_tensor // self.nx
        shifts = [(x, y) for y in range(self.ny) for x in range(self.nx)]
        self.shifts = sorted(shifts, key=lambda xy: ((xy[0] > 0) + (xy[1] > 0), xy[1], xy[0]))
        self.along_x = [j for j, (x, y) in enumerate(self.shifts) if x and not y]
        self.along_y = [j for j, (x, y) in enumerate(self.shifts) if y and not x]
        self.far = [j for j, (x, y) in enumerate(self.shifts) if x and y]
        self.cap = min(rows, max(2, 2 * rows // n_dp))
        self.whole = self.cap // 16 * 16
        self.rest = self.cap - self.whole
        self.cols = emb // CHUNKS
        self.tiles = self.cols // 128
        self.folded = -(-self.rest * self.tiles // 16) * 16
        self.block = self.whole * self.tiles + self.folded
        self.slots = n_dp * self.cap
        self.lanes = -(-self.slots // 128) * 128


def kernel(
    z,
    features,
    w_hidden,
    w_embed,
    members,
    hbm_owner,
    hbm_local,
    hbm_cluster,
    hbm_valid,
    best,
    feat,
    w1,
    w2,
    raw,
    doc_owner,
    doc_local,
    member_cluster,
    member_valid,
    unit,
    member_tag,
    sums_out,
    sums_in,
    docs_out,
    docs_in,
    tags_out,
    tags_in,
    answer_out,
    answer_in,
    local_sem,
    feat_send,
    feat_recv,
    unit_send,
    unit_recv,
    mtag_send,
    mtag_recv,
    sums_send,
    sums_recv,
    docs_send,
    docs_recv,
    tags_send,
    tags_recv,
    answer_send,
    answer_recv,
):
    p = lax.axis_index("dp")
    t = lax.axis_index("tensor")
    tx, ty = lax.rem(t, z.nx), lax.div(t, z.nx)
    half = z.hid // 2
    sent = []

    def forward_of(j):
        dx, dy = z.shifts[j]
        return lax.rem(ty + dy, z.ny) * z.nx + lax.rem(tx + dx, z.nx)

    def source_of(j):
        dx, dy = z.shifts[j]
        return lax.rem(ty + z.ny - dy, z.ny) * z.nx + lax.rem(tx + z.nx - dx, z.nx)

    def remote(src, dst, send, recv, **device):
        copy = pltpu.make_async_remote_copy(
            src_ref=src, dst_ref=dst, send_sem=send, recv_sem=recv, device_id=device,
            device_id_type=MESH,
        )
        copy.start()
        sent.append(copy)
        return copy

    barrier = pltpu.get_barrier_semaphore()
    for j in range(1, z.n_tensor):
        pl.semaphore_signal(barrier, inc=1, device_id={"tensor": forward_of(j)}, device_id_type=MESH)
    for k in range(1, z.n_dp):
        pl.semaphore_signal(
            barrier, inc=1, device_id={"dp": lax.rem(p + k, z.n_dp)}, device_id_type=MESH
        )

    own = [
        pltpu.make_async_copy(features.at[:, pl.ds(h * half, half)], feat.at[h, 0], local_sem.at[h])
        for h in (0, 1)
    ]
    load_w1 = [
        pltpu.make_async_copy(
            w_hidden.at[pl.ds(h * half, half)], w1.at[pl.ds(h * half, half)], local_sem.at[2 + h]
        )
        for h in (0, 1)
    ]
    load_w2 = pltpu.make_async_copy(w_embed, w2, local_sem.at[4])
    load_members = pltpu.make_async_copy(members.at[0], raw, local_sem.at[5])
    load_small = [
        pltpu.make_async_copy(src, dst, local_sem.at[6 + i])
        for i, (src, dst) in enumerate(
            (
                (hbm_owner, doc_owner),
                (hbm_local, doc_local),
                (hbm_cluster, member_cluster),
                (hbm_valid, member_valid),
            )
        )
    ]
    for copy in (*load_small, *own, *load_w1, load_w2, load_members):
        copy.start()

    pl.semaphore_wait(barrier, z.n_tensor - 1 + z.n_dp - 1)

    feat_copy = {}

    def send_feature(h, j, src, target):
        feat_copy[h, j] = remote(
            src, feat.at[h, j], feat_send.at[h, j], feat_recv.at[h, j], tensor=forward_of(target)
        )

    along_x, along_y, far = z.along_x, z.along_y, z.far

    def corner(x, y):
        return z.shifts.index((z.shifts[x][0], z.shifts[y][1]))

    for first in (0, 1):
        for j in along_x:
            h = first
            send_feature(h, j, features.at[:, pl.ds(h * half, half)], j)
        for j in along_y:
            h = 1 - first
            send_feature(h, j, features.at[:, pl.ds(h * half, half)], j)

    for copy in load_small:
        copy.wait()
    rows, wide = z.rows, doc_owner.shape[1]
    mine = iota((rows, wide), 1) == iota((rows, wide), 0) + (t * rows).astype(F32)
    owner = jnp.sum(jnp.where(mine, doc_owner[...].astype(F32), 0.0), axis=1, keepdims=True)
    local = jnp.sum(jnp.where(mine, doc_local[...].reshape(1, wide).astype(F32), 0.0), axis=1, keepdims=True)
    step = owner - p.astype(F32)
    step = jnp.where(step < 0.0, step + float(z.n_dp), step)
    step_row = to_row(step, rows)
    same = step == step_row
    above = iota((rows, rows), 0)
    across = iota((rows, rows), 1)
    rank = jnp.sum(jnp.where(same & (across < above), 1.0, 0.0), axis=1, keepdims=True)
    rank_row = jnp.sum(jnp.where(same & (above < across), 1.0, 0.0), axis=0, keepdims=True)
    place = jnp.where(
        rank < float(z.whole),
        step * float(z.whole) + rank,
        float(z.n_dp * z.whole) + step * float(z.rest) + rank - float(z.whole),
    )
    placed = iota((rows, z.lanes), 1) == place
    step_hot = jnp.where(iota((z.n_dp, rows), 0) == step_row, 1.0, 0.0).astype(BF16)
    tags = jnp.dot(
        step_hot,
        jnp.where(placed, local + 1.0, 0.0).astype(BF16),
        preferred_element_type=F32,
    )
    for k in range(z.n_dp):
        tags_out[k] = tags[k : k + 1, :]
    tags_copy = [
        remote(
            tags_out.at[k], tags_in.at[k], tags_send.at[k], tags_recv.at[k],
            dp=lax.rem(p + k, z.n_dp),
        )
        for k in range(1, z.n_dp)
    ]

    member_tag[0] = jnp.where(
        member_valid[...] == 1, member_cluster[...].astype(F32) + 1.0, -1.0
    )
    load_members.wait()
    values = raw[...].astype(F32)
    unit[:, 0] = (
        (values / jnp.sqrt(jnp.sum(values * values, axis=1, keepdims=True) + EPSILON))
        .astype(BF16)
        .reshape(2, z.members // 2, z.emb)
    )
    mtag_copy = [
        remote(
            member_tag.at[0], member_tag.at[j], mtag_send.at[j], mtag_recv.at[j],
            tensor=forward_of(j),
        )
        for j in range(1, z.n_tensor)
    ]

    def head(first, last):
        count = last - first
        total = jnp.dot(
            feat[0, first:last].reshape(count * z.rows, half),
            w1[:half, :],
            preferred_element_type=F32,
        )
        total += jnp.dot(
            feat[1, first:last].reshape(count * z.rows, half),
            w1[half:, :],
            preferred_element_type=F32,
        )
        hidden = jax.nn.gelu(total).astype(BF16)
        for c in range(CHUNKS):
            sums_out[c, first:last] = (
                jnp.dot(
                    hidden, w2[:, c * z.cols : (c + 1) * z.cols], preferred_element_type=F32
                )
                .astype(BF16)
                .reshape(count, z.rows, z.cols)
            )
            for j in range(max(first, 1), last):
                sums_copy[c, j] = remote(
                    sums_out.at[c, j], sums_in.at[c, j], sums_send.at[c, j], sums_recv.at[c, j],
                    tensor=source_of(j),
                )

    sums_copy = {}
    for copy in (*own, *load_w1, load_w2):
        copy.wait()
    head(0, 1)

    for j in along_x:
        feat_copy[0, j].wait_recv()
        for y in along_y:
            send_feature(0, corner(j, y), feat.at[0, j], y)
    for j in along_y:
        feat_copy[1, j].wait_recv()
        for x in along_x:
            send_feature(1, corner(x, j), feat.at[1, j], x)
    for j in along_x:
        feat_copy[1, j].wait_recv()
    for j in along_y:
        feat_copy[0, j].wait_recv()
    head(1, 1 + len(along_x) + len(along_y))
    for j in far:
        feat_copy[0, j].wait_recv()
        feat_copy[1, j].wait_recv()

    unit_copy = {}

    def send_unit(h, j, held, target):
        unit_copy[h, j] = remote(
            unit.at[h, held], unit.at[h, j], unit_send.at[h, j], unit_recv.at[h, j],
            tensor=forward_of(target),
        )

    for first in (0, 1):
        for j in along_x:
            send_unit(first, j, 0, j)
        for j in along_y:
            send_unit(1 - first, j, 0, j)
    if far:
        head(far[0], far[-1] + 1)

    code = step_row * float(z.cap) + rank_row
    code = code.reshape(1, 1, rows)
    if z.whole:
        shape = (z.n_dp, z.whole, rows)
        pack_whole = jnp.where(
            code == iota(shape, 0) * float(z.cap) + iota(shape, 1), 1.0, 0.0
        ).reshape(z.n_dp * z.whole, rows).astype(BF16)
    pack_rest = []
    if z.rest:
        shape = (z.n_dp, z.folded, rows)
        for c in range(z.tiles):
            at = iota(shape, 1) - float(c * z.rest)
            inside = (at >= 0.0) & (at < float(z.rest))
            hit = inside & (code == iota(shape, 0) * float(z.cap) + float(z.whole) + at)
            pack_rest.append(
                jnp.where(hit, 1.0, 0.0).reshape(z.n_dp * z.folded, rows).astype(BF16)
            )

    square = jnp.zeros((rows, 1), F32)
    docs_copy = {}
    for c in range(CHUNKS):
        proj = sums_out[c, 0].astype(F32)
        for j in range(1, z.n_tensor):
            sums_copy[c, j].wait_recv()
            proj += sums_in[c, j].astype(F32)
        query = proj.astype(BF16)
        if z.whole:
            packed = jnp.dot(pack_whole, query, preferred_element_type=F32).astype(BF16)
        if z.rest:
            tail = jnp.zeros((z.n_dp * z.folded, 128), F32)
            for i in range(z.tiles):
                tail += jnp.dot(
                    pack_rest[i], query[:, i * 128 : (i + 1) * 128], preferred_element_type=F32
                )
            tail = tail.astype(BF16)
        for k in [*range(1, z.n_dp), 0]:
            target = docs_out if k else docs_in
            if z.whole:
                for i in range(z.tiles):
                    target[c, k, i * z.whole : (i + 1) * z.whole, :] = packed[
                        k * z.whole : (k + 1) * z.whole, i * 128 : (i + 1) * 128
                    ]
            if z.rest:
                target[c, k, z.tiles * z.whole :, :] = tail[k * z.folded : (k + 1) * z.folded, :]
            if k:
                docs_copy[c, k] = remote(
                    docs_out.at[c, k], docs_in.at[c, k], docs_send.at[c, k], docs_recv.at[c, k],
                    dp=lax.rem(p + k, z.n_dp),
                )
        square += jnp.sum(proj * proj, axis=1, keepdims=True)
    inverse = 1.0 / jnp.sqrt(square + EPSILON)
    for j in along_x:
        unit_copy[0, j].wait_recv()
        for y in along_y:
            send_unit(0, corner(j, y), j, y)
    for j in along_y:
        unit_copy[1, j].wait_recv()
        for x in along_x:
            send_unit(1, corner(x, j), j, x)

    tag_row = tags_out[0]
    for k in range(1, z.n_dp):
        tags_copy[k - 1].wait_recv()
        tag_row += tags_in[k]
    tag_row = tag_row[:, : z.slots]
    for copy in mtag_copy:
        copy.wait_recv()
    allowed = [to_column(member_tag[j], z.members) for j in range(z.n_tensor)]

    unfold = []
    if z.rest:
        shape = (z.n_dp * z.rest, z.n_dp * z.folded)
        out_row, in_row = iota(shape, 0), iota(shape, 1)
        for i in range(z.tiles):
            hit = jnp.zeros(shape, F32)
            for k in range(z.n_dp):
                at = out_row - float(k * z.rest)
                inside = (at >= 0.0) & (at < float(z.rest))
                hit = jnp.where(
                    inside & (in_row == at + float(k * z.folded + i * z.rest)), 1.0, hit
                )
            unfold.append(hit.astype(BF16))

    arrived = []
    for c in range(CHUNKS):
        for k in range(1, z.n_dp):
            docs_copy[c, k].wait_recv()
        parts = []
        if z.whole:
            parts.append(
                jnp.concatenate(
                    [
                        docs_in[c, :, i * z.whole : (i + 1) * z.whole, :].reshape(
                            z.n_dp * z.whole, 128
                        )
                        for i in range(z.tiles)
                    ],
                    axis=1,
                )
            )
        if z.rest:
            tail = docs_in[c, :, z.tiles * z.whole :, :].reshape(z.n_dp * z.folded, 128)
            parts.append(
                jnp.concatenate(
                    [
                        jnp.dot(unfold[i], tail, preferred_element_type=F32).astype(BF16)
                        for i in range(z.tiles)
                    ],
                    axis=1,
                )
            )
        arrived.append(jnp.concatenate(parts, axis=0) if len(parts) > 1 else parts[0])
    top = jnp.full((1, z.slots), LOWEST, F32)
    for j in range(z.n_tensor):
        if j in along_x:
            unit_copy[1, j].wait_recv()
        elif j in along_y:
            unit_copy[0, j].wait_recv()
        elif j:
            unit_copy[0, j].wait_recv()
            unit_copy[1, j].wait_recv()
        scores = jnp.zeros((z.members, z.slots), F32)
        for c in range(CHUNKS):
            scores += lax.dot_general(
                unit[:, j, :, c * z.cols : (c + 1) * z.cols].reshape(z.members, z.cols),
                arrived[c],
                (((1,), (1,)), ((), ())),
                preferred_element_type=F32,
            )
        kept = jnp.where(allowed[j] == tag_row, scores, LOWEST)
        top = jnp.maximum(top, jnp.max(kept, axis=0, keepdims=True))
    answer_out[...] = jnp.zeros_like(answer_out)
    answer_out[:, : z.slots] = top

    answer_copy = [
        remote(
            answer_out, answer_in.at[k], answer_send.at[k], answer_recv.at[k],
            dp=lax.rem(p + z.n_dp - k, z.n_dp),
        )
        for k in range(1, z.n_dp)
    ]
    found = jnp.where(step == 0.0, answer_out[...], 0.0)
    for k in range(1, z.n_dp):
        answer_copy[k - 1].wait_recv()
        found = jnp.where(step == float(k), answer_in[k], found)
    value = jnp.sum(jnp.where(placed, found, 0.0), axis=1, keepdims=True)
    best[...] = to_row(jnp.maximum(value * inverse, -1.0), rows)
    for copy in sent:
        copy.wait_send()


def body(features, w_hidden, w_embed, members, doc_owner, doc_local, member_cluster, member_valid):
    n_dp, n_tensor = lax.axis_size("dp"), lax.axis_size("tensor")
    rows, hid = features.shape
    width, emb = w_embed.shape
    z = Sizes(n_dp, n_tensor, rows, hid, width, emb, members.shape[1])
    half = hid // 2
    dma = pltpu.SemaphoreType.DMA
    hbm = pl.BlockSpec(memory_space=pl.ANY)
    vmem = pl.BlockSpec(memory_space=pltpu.VMEM)
    out = pl.pallas_call(
        functools.partial(kernel, z),
        out_shape=jax.ShapeDtypeStruct((1, rows), F32),
        in_specs=[hbm] * 8,
        out_specs=vmem,
        scratch_shapes=[
            pltpu.VMEM((2, n_tensor, rows, half), BF16),
            pltpu.VMEM((hid, width), BF16),
            pltpu.VMEM((width, emb), BF16),
            pltpu.VMEM((z.members, emb), BF16),
            pltpu.VMEM((1, doc_owner.shape[0]), jnp.int32),
            pltpu.VMEM(doc_local.shape, jnp.int32),
            pltpu.VMEM((1, z.members), jnp.int32),
            pltpu.VMEM((1, z.members), jnp.int32),
            pltpu.VMEM((2, n_tensor, z.members // 2, emb), BF16),
            pltpu.VMEM((n_tensor, 1, z.members), F32),
            pltpu.VMEM((CHUNKS, n_tensor, rows, z.cols), BF16),
            pltpu.VMEM((CHUNKS, n_tensor, rows, z.cols), BF16),
            pltpu.VMEM((CHUNKS, n_dp, z.block, 128), BF16),
            pltpu.VMEM((CHUNKS, n_dp, z.block, 128), BF16),
            pltpu.VMEM((n_dp, 1, z.lanes), F32),
            pltpu.VMEM((n_dp, 1, z.lanes), F32),
            pltpu.VMEM((1, z.lanes), F32),
            pltpu.VMEM((n_dp, 1, z.lanes), F32),
            dma((10,)),
            dma((2, n_tensor)),
            dma((2, n_tensor)),
            dma((2, n_tensor)),
            dma((2, n_tensor)),
            dma((n_tensor,)),
            dma((n_tensor,)),
            dma((CHUNKS, n_tensor)),
            dma((CHUNKS, n_tensor)),
            dma((CHUNKS, n_dp)),
            dma((CHUNKS, n_dp)),
            dma((n_dp,)),
            dma((n_dp,)),
            dma((n_dp,)),
            dma((n_dp,)),
        ],
        compiler_params=pltpu.CompilerParams(
            collective_id=0, has_side_effects=True, vmem_limit_bytes=62 * 1024 * 1024
        ),
        name="match",
    )(
        features,
        w_hidden,
        w_embed,
        members,
        doc_owner.reshape(1, -1),
        doc_local,
        member_cluster,
        member_valid,
    )
    return out.reshape(rows)


def solution(mesh):
    return jax.shard_map(
        body,
        mesh=mesh,
        in_specs=(
            P(("dp", "tensor"), None),
            P(None, "tensor"),
            P("tensor", None),
            P("dp", "tensor", None),
            P("dp", None),
            P("dp"),
            P("dp", "tensor"),
            P("dp", "tensor"),
        ),
        out_specs=P(("dp", "tensor")),
        check_vma=False,
    )
```

```python
import functools
import math

import jax
import jax.numpy as jnp
from jax import lax
from jax.experimental import pallas as pl
from jax.experimental.pallas import tpu as pltpu
from jax.sharding import PartitionSpec as P

EPSILON = 1e-06
MESH = pl.DeviceIdType.MESH
F32 = jnp.float32
BF16 = jnp.bfloat16
LOWEST = -1e30
CHUNKS = 2


def iota(shape, dim):
    return lax.broadcasted_iota(jnp.int32, shape, dim).astype(F32)


def to_column(row, size):
    eye = iota((size, size), 0) == iota((size, size), 1)
    return jnp.sum(jnp.where(eye, row, 0.0), axis=1, keepdims=True)


def to_row(column, size):
    eye = iota((size, size), 0) == iota((size, size), 1)
    return jnp.sum(jnp.where(eye, column, 0.0), axis=0, keepdims=True)


class Sizes:
    def __init__(self, n_dp, n_tensor, rows, hid, width, emb, members):
        self.n_dp, self.n_tensor = n_dp, n_tensor
        self.rows, self.hid, self.width, self.emb, self.members = rows, hid, width, emb, members
        self.nx = max(d for d in range(1, math.isqrt(n_tensor) + 1) if n_tensor % d == 0)
        self.ny = n_tensor // self.nx
        shifts = [(x, y) for y in range(self.ny) for x in range(self.nx)]
        self.shifts = sorted(shifts, key=lambda xy: ((xy[0] > 0) + (xy[1] > 0), xy[1], xy[0]))
        self.along_x = [j for j, (x, y) in enumerate(self.shifts) if x and not y]
        self.along_y = [j for j, (x, y) in enumerate(self.shifts) if y and not x]
        self.far = [j for j, (x, y) in enumerate(self.shifts) if x and y]
        self.cap = min(rows, max(2, 2 * rows // n_dp))
        self.whole = self.cap // 16 * 16
        self.rest = self.cap - self.whole
        self.cols = emb // CHUNKS
        self.tiles = self.cols // 128
        self.folded = -(-self.rest * self.tiles // 16) * 16
        self.block = self.whole * self.tiles + self.folded
        self.slots = n_dp * self.cap
        self.lanes = -(-self.slots // 128) * 128


def kernel(
    z,
    features,
    w_hidden,
    w_embed,
    members,
    hbm_owner,
    hbm_local,
    hbm_cluster,
    hbm_valid,
    best,
    feat,
    w1,
    w2,
    raw,
    doc_owner,
    doc_local,
    member_cluster,
    member_valid,
    unit,
    member_tag,
    sums_out,
    sums_in,
    docs_out,
    docs_in,
    tags_out,
    tags_in,
    answer_out,
    answer_in,
    local_sem,
    feat_send,
    feat_recv,
    unit_send,
    unit_recv,
    mtag_send,
    mtag_recv,
    sums_send,
    sums_recv,
    docs_send,
    docs_recv,
    tags_send,
    tags_recv,
    answer_send,
    answer_recv,
):
    p = lax.axis_index("dp")
    t = lax.axis_index("tensor")
    tx, ty = lax.rem(t, z.nx), lax.div(t, z.nx)
    half = z.hid // 2
    sent = []

    def forward_of(j):
        dx, dy = z.shifts[j]
        return lax.rem(ty + dy, z.ny) * z.nx + lax.rem(tx + dx, z.nx)

    def source_of(j):
        dx, dy = z.shifts[j]
        return lax.rem(ty + z.ny - dy, z.ny) * z.nx + lax.rem(tx + z.nx - dx, z.nx)

    def remote(src, dst, send, recv, **device):
        copy = pltpu.make_async_remote_copy(
            src_ref=src, dst_ref=dst, send_sem=send, recv_sem=recv, device_id=device,
            device_id_type=MESH,
        )
        copy.start()
        sent.append(copy)
        return copy

    barrier = pltpu.get_barrier_semaphore()
    for j in range(1, z.n_tensor):
        pl.semaphore_signal(barrier, inc=1, device_id={"tensor": forward_of(j)}, device_id_type=MESH)
    for k in range(1, z.n_dp):
        pl.semaphore_signal(
            barrier, inc=1, device_id={"dp": lax.rem(p + k, z.n_dp)}, device_id_type=MESH
        )

    own = [
        pltpu.make_async_copy(features.at[:, pl.ds(h * half, half)], feat.at[h, 0], local_sem.at[h])
        for h in (0, 1)
    ]
    load_w1 = [
        pltpu.make_async_copy(
            w_hidden.at[pl.ds(h * half, half)], w1.at[pl.ds(h * half, half)], local_sem.at[2 + h]
        )
        for h in (0, 1)
    ]
    load_w2 = pltpu.make_async_copy(w_embed, w2, local_sem.at[4])
    load_members = pltpu.make_async_copy(members.at[0], raw, local_sem.at[5])
    load_small = [
        pltpu.make_async_copy(src, dst, local_sem.at[6 + i])
        for i, (src, dst) in enumerate(
            (
                (hbm_owner, doc_owner),
                (hbm_local, doc_local),
                (hbm_cluster, member_cluster),
                (hbm_valid, member_valid),
            )
        )
    ]
    for copy in (*load_small, *own, *load_w1, load_w2, load_members):
        copy.start()

    pl.semaphore_wait(barrier, z.n_tensor - 1 + z.n_dp - 1)

    feat_copy = {}

    def send_feature(h, j, src, target):
        feat_copy[h, j] = remote(
            src, feat.at[h, j], feat_send.at[h, j], feat_recv.at[h, j], tensor=forward_of(target)
        )

    along_x, along_y, far = z.along_x, z.along_y, z.far

    def corner(x, y):
        return z.shifts.index((z.shifts[x][0], z.shifts[y][1]))

    for first in (0, 1):
        for j in along_x:
            h = first
            send_feature(h, j, features.at[:, pl.ds(h * half, half)], j)
        for j in along_y:
            h = 1 - first
            send_feature(h, j, features.at[:, pl.ds(h * half, half)], j)

    for copy in load_small:
        copy.wait()
    rows, wide = z.rows, doc_owner.shape[1]
    mine = iota((rows, wide), 1) == iota((rows, wide), 0) + (t * rows).astype(F32)
    owner = jnp.sum(jnp.where(mine, doc_owner[...].astype(F32), 0.0), axis=1, keepdims=True)
    local = jnp.sum(jnp.where(mine, doc_local[...].reshape(1, wide).astype(F32), 0.0), axis=1, keepdims=True)
    step = owner - p.astype(F32)
    step = jnp.where(step < 0.0, step + float(z.n_dp), step)
    step_row = to_row(step, rows)
    same = step == step_row
    above = iota((rows, rows), 0)
    across = iota((rows, rows), 1)
    rank = jnp.sum(jnp.where(same & (across < above), 1.0, 0.0), axis=1, keepdims=True)
    rank_row = jnp.sum(jnp.where(same & (above < across), 1.0, 0.0), axis=0, keepdims=True)
    place = jnp.where(
        rank < float(z.whole),
        step * float(z.whole) + rank,
        float(z.n_dp * z.whole) + step * float(z.rest) + rank - float(z.whole),
    )
    placed = iota((rows, z.lanes), 1) == place
    step_hot = jnp.where(iota((z.n_dp, rows), 0) == step_row, 1.0, 0.0).astype(BF16)
    tags = jnp.dot(
        step_hot,
        jnp.where(placed, local + 1.0, 0.0).astype(BF16),
        preferred_element_type=F32,
    )
    for k in range(z.n_dp):
        tags_out[k] = tags[k : k + 1, :]
    tags_copy = [
        remote(
            tags_out.at[k], tags_in.at[k], tags_send.at[k], tags_recv.at[k],
            dp=lax.rem(p + k, z.n_dp),
        )
        for k in range(1, z.n_dp)
    ]

    member_tag[0] = jnp.where(
        member_valid[...] == 1, member_cluster[...].astype(F32) + 1.0, -1.0
    )
    load_members.wait()
    values = raw[...].astype(F32)
    unit[:, 0] = (
        (values / jnp.sqrt(jnp.sum(values * values, axis=1, keepdims=True) + EPSILON))
        .astype(BF16)
        .reshape(2, z.members // 2, z.emb)
    )
    mtag_copy = [
        remote(
            member_tag.at[0], member_tag.at[j], mtag_send.at[j], mtag_recv.at[j],
            tensor=forward_of(j),
        )
        for j in range(1, z.n_tensor)
    ]

    def head(first, last):
        count = last - first
        total = jnp.dot(
            feat[0, first:last].reshape(count * z.rows, half),
            w1[:half, :],
            preferred_element_type=F32,
        )
        total += jnp.dot(
            feat[1, first:last].reshape(count * z.rows, half),
            w1[half:, :],
            preferred_element_type=F32,
        )
        hidden = jax.nn.gelu(total).astype(BF16)
        for c in range(CHUNKS):
            sums_out[c, first:last] = (
                jnp.dot(
                    hidden, w2[:, c * z.cols : (c + 1) * z.cols], preferred_element_type=F32
                )
                .astype(BF16)
                .reshape(count, z.rows, z.cols)
            )
            for j in range(max(first, 1), last):
                sums_copy[c, j] = remote(
                    sums_out.at[c, j], sums_in.at[c, j], sums_send.at[c, j], sums_recv.at[c, j],
                    tensor=source_of(j),
                )

    sums_copy = {}
    for copy in (*own, *load_w1, load_w2):
        copy.wait()
    head(0, 1)

    for j in along_x:
        feat_copy[0, j].wait_recv()
        for y in along_y:
            send_feature(0, corner(j, y), feat.at[0, j], y)
    for j in along_y:
        feat_copy[1, j].wait_recv()
        for x in along_x:
            send_feature(1, corner(x, j), feat.at[1, j], x)
    for j in along_x:
        feat_copy[1, j].wait_recv()
    for j in along_y:
        feat_copy[0, j].wait_recv()
    head(1, 1 + len(along_x) + len(along_y))
    for j in far:
        feat_copy[0, j].wait_recv()
        feat_copy[1, j].wait_recv()

    unit_copy = {}

    def send_unit(h, j, held, target):
        unit_copy[h, j] = remote(
            unit.at[h, held], unit.at[h, j], unit_send.at[h, j], unit_recv.at[h, j],
            tensor=forward_of(target),
        )

    if far:
        head(far[0], far[-1] + 1)

    code = step_row * float(z.cap) + rank_row
    code = code.reshape(1, 1, rows)
    if z.whole:
        shape = (z.n_dp, z.whole, rows)
        pack_whole = jnp.where(
            code == iota(shape, 0) * float(z.cap) + iota(shape, 1), 1.0, 0.0
        ).reshape(z.n_dp * z.whole, rows).astype(BF16)
    pack_rest = []
    if z.rest:
        shape = (z.n_dp, z.folded, rows)
        for c in range(z.tiles):
            at = iota(shape, 1) - float(c * z.rest)
            inside = (at >= 0.0) & (at < float(z.rest))
            hit = inside & (code == iota(shape, 0) * float(z.cap) + float(z.whole) + at)
            pack_rest.append(
                jnp.where(hit, 1.0, 0.0).reshape(z.n_dp * z.folded, rows).astype(BF16)
            )

    square = jnp.zeros((rows, 1), F32)
    docs_copy = {}
    for c in range(CHUNKS):
        proj = sums_out[c, 0].astype(F32)
        for j in range(1, z.n_tensor):
            sums_copy[c, j].wait_recv()
            proj += sums_in[c, j].astype(F32)
        query = proj.astype(BF16)
        if z.whole:
            packed = jnp.dot(pack_whole, query, preferred_element_type=F32).astype(BF16)
        if z.rest:
            tail = jnp.zeros((z.n_dp * z.folded, 128), F32)
            for i in range(z.tiles):
                tail += jnp.dot(
                    pack_rest[i], query[:, i * 128 : (i + 1) * 128], preferred_element_type=F32
                )
            tail = tail.astype(BF16)
        for k in [*range(1, z.n_dp), 0]:
            target = docs_out if k else docs_in
            if z.whole:
                for i in range(z.tiles):
                    target[c, k, i * z.whole : (i + 1) * z.whole, :] = packed[
                        k * z.whole : (k + 1) * z.whole, i * 128 : (i + 1) * 128
                    ]
            if z.rest:
                target[c, k, z.tiles * z.whole :, :] = tail[k * z.folded : (k + 1) * z.folded, :]
            if k:
                docs_copy[c, k] = remote(
                    docs_out.at[c, k], docs_in.at[c, k], docs_send.at[c, k], docs_recv.at[c, k],
                    dp=lax.rem(p + k, z.n_dp),
                )
        square += jnp.sum(proj * proj, axis=1, keepdims=True)
    for first in (0, 1):
        for j in along_x:
            send_unit(first, j, 0, j)
        for j in along_y:
            send_unit(1 - first, j, 0, j)
    inverse = 1.0 / jnp.sqrt(square + EPSILON)
    for j in along_x:
        unit_copy[0, j].wait_recv()
        for y in along_y:
            send_unit(0, corner(j, y), j, y)
    for j in along_y:
        unit_copy[1, j].wait_recv()
        for x in along_x:
            send_unit(1, corner(x, j), j, x)

    tag_row = tags_out[0]
    for k in range(1, z.n_dp):
        tags_copy[k - 1].wait_recv()
        tag_row += tags_in[k]
    tag_row = tag_row[:, : z.slots]
    for copy in mtag_copy:
        copy.wait_recv()
    allowed = [to_column(member_tag[j], z.members) for j in range(z.n_tensor)]

    unfold = []
    if z.rest:
        shape = (z.n_dp * z.rest, z.n_dp * z.folded)
        out_row, in_row = iota(shape, 0), iota(shape, 1)
        for i in range(z.tiles):
            hit = jnp.zeros(shape, F32)
            for k in range(z.n_dp):
                at = out_row - float(k * z.rest)
                inside = (at >= 0.0) & (at < float(z.rest))
                hit = jnp.where(
                    inside & (in_row == at + float(k * z.folded + i * z.rest)), 1.0, hit
                )
            unfold.append(hit.astype(BF16))

    arrived = []
    for c in range(CHUNKS):
        for k in range(1, z.n_dp):
            docs_copy[c, k].wait_recv()
        parts = []
        if z.whole:
            parts.append(
                jnp.concatenate(
                    [
                        docs_in[c, :, i * z.whole : (i + 1) * z.whole, :].reshape(
                            z.n_dp * z.whole, 128
                        )
                        for i in range(z.tiles)
                    ],
                    axis=1,
                )
            )
        if z.rest:
            tail = docs_in[c, :, z.tiles * z.whole :, :].reshape(z.n_dp * z.folded, 128)
            parts.append(
                jnp.concatenate(
                    [
                        jnp.dot(unfold[i], tail, preferred_element_type=F32).astype(BF16)
                        for i in range(z.tiles)
                    ],
                    axis=1,
                )
            )
        arrived.append(jnp.concatenate(parts, axis=0) if len(parts) > 1 else parts[0])
    top = jnp.full((1, z.slots), LOWEST, F32)
    for j in range(z.n_tensor):
        if j in along_x:
            unit_copy[1, j].wait_recv()
        elif j in along_y:
            unit_copy[0, j].wait_recv()
        elif j:
            unit_copy[0, j].wait_recv()
            unit_copy[1, j].wait_recv()
        scores = jnp.zeros((z.members, z.slots), F32)
        for c in range(CHUNKS):
            scores += lax.dot_general(
                unit[:, j, :, c * z.cols : (c + 1) * z.cols].reshape(z.members, z.cols),
                arrived[c],
                (((1,), (1,)), ((), ())),
                preferred_element_type=F32,
            )
        kept = jnp.where(allowed[j] == tag_row, scores, LOWEST)
        top = jnp.maximum(top, jnp.max(kept, axis=0, keepdims=True))
    answer_out[...] = jnp.zeros_like(answer_out)
    answer_out[:, : z.slots] = top

    answer_copy = [
        remote(
            answer_out, answer_in.at[k], answer_send.at[k], answer_recv.at[k],
            dp=lax.rem(p + z.n_dp - k, z.n_dp),
        )
        for k in range(1, z.n_dp)
    ]
    found = jnp.where(step == 0.0, answer_out[...], 0.0)
    for k in range(1, z.n_dp):
        answer_copy[k - 1].wait_recv()
        found = jnp.where(step == float(k), answer_in[k], found)
    value = jnp.sum(jnp.where(placed, found, 0.0), axis=1, keepdims=True)
    best[...] = to_row(jnp.maximum(value * inverse, -1.0), rows)
    for copy in sent:
        copy.wait_send()


def body(features, w_hidden, w_embed, members, doc_owner, doc_local, member_cluster, member_valid):
    n_dp, n_tensor = lax.axis_size("dp"), lax.axis_size("tensor")
    rows, hid = features.shape
    width, emb = w_embed.shape
    z = Sizes(n_dp, n_tensor, rows, hid, width, emb, members.shape[1])
    half = hid // 2
    dma = pltpu.SemaphoreType.DMA
    hbm = pl.BlockSpec(memory_space=pl.ANY)
    vmem = pl.BlockSpec(memory_space=pltpu.VMEM)
    out = pl.pallas_call(
        functools.partial(kernel, z),
        out_shape=jax.ShapeDtypeStruct((1, rows), F32),
        in_specs=[hbm] * 8,
        out_specs=vmem,
        scratch_shapes=[
            pltpu.VMEM((2, n_tensor, rows, half), BF16),
            pltpu.VMEM((hid, width), BF16),
            pltpu.VMEM((width, emb), BF16),
            pltpu.VMEM((z.members, emb), BF16),
            pltpu.VMEM((1, doc_owner.shape[0]), jnp.int32),
            pltpu.VMEM(doc_local.shape, jnp.int32),
            pltpu.VMEM((1, z.members), jnp.int32),
            pltpu.VMEM((1, z.members), jnp.int32),
            pltpu.VMEM((2, n_tensor, z.members // 2, emb), BF16),
            pltpu.VMEM((n_tensor, 1, z.members), F32),
            pltpu.VMEM((CHUNKS, n_tensor, rows, z.cols), BF16),
            pltpu.VMEM((CHUNKS, n_tensor, rows, z.cols), BF16),
            pltpu.VMEM((CHUNKS, n_dp, z.block, 128), BF16),
            pltpu.VMEM((CHUNKS, n_dp, z.block, 128), BF16),
            pltpu.VMEM((n_dp, 1, z.lanes), F32),
            pltpu.VMEM((n_dp, 1, z.lanes), F32),
            pltpu.VMEM((1, z.lanes), F32),
            pltpu.VMEM((n_dp, 1, z.lanes), F32),
            dma((10,)),
            dma((2, n_tensor)),
            dma((2, n_tensor)),
            dma((2, n_tensor)),
            dma((2, n_tensor)),
            dma((n_tensor,)),
            dma((n_tensor,)),
            dma((CHUNKS, n_tensor)),
            dma((CHUNKS, n_tensor)),
            dma((CHUNKS, n_dp)),
            dma((CHUNKS, n_dp)),
            dma((n_dp,)),
            dma((n_dp,)),
            dma((n_dp,)),
            dma((n_dp,)),
        ],
        compiler_params=pltpu.CompilerParams(
            collective_id=0, has_side_effects=True, vmem_limit_bytes=62 * 1024 * 1024
        ),
        name="match",
    )(
        features,
        w_hidden,
        w_embed,
        members,
        doc_owner.reshape(1, -1),
        doc_local,
        member_cluster,
        member_valid,
    )
    return out.reshape(rows)


def solution(mesh):
    return jax.shard_map(
        body,
        mesh=mesh,
        in_specs=(
            P(("dp", "tensor"), None),
            P(None, "tensor"),
            P("tensor", None),
            P("dp", "tensor", None),
            P("dp", None),
            P("dp"),
            P("dp", "tensor"),
            P("dp", "tensor"),
        ),
        out_specs=P(("dp", "tensor")),
        check_vma=False,
    )
```

```python
import functools
import math

import jax
import jax.numpy as jnp
from jax import lax
from jax.experimental import pallas as pl
from jax.experimental.pallas import tpu as pltpu
from jax.sharding import PartitionSpec as P

EPSILON = 1e-06
MESH = pl.DeviceIdType.MESH
F32 = jnp.float32
BF16 = jnp.bfloat16
LOWEST = -1e30
CHUNKS = 2


def iota(shape, dim):
    return lax.broadcasted_iota(jnp.int32, shape, dim).astype(F32)


def to_column(row, size):
    eye = iota((size, size), 0) == iota((size, size), 1)
    return jnp.sum(jnp.where(eye, row, 0.0), axis=1, keepdims=True)


def to_row(column, size):
    eye = iota((size, size), 0) == iota((size, size), 1)
    return jnp.sum(jnp.where(eye, column, 0.0), axis=0, keepdims=True)


class Sizes:
    def __init__(self, n_dp, n_tensor, rows, hid, width, emb, members):
        self.n_dp, self.n_tensor = n_dp, n_tensor
        self.rows, self.hid, self.width, self.emb, self.members = rows, hid, width, emb, members
        self.nx = max(d for d in range(1, math.isqrt(n_tensor) + 1) if n_tensor % d == 0)
        self.ny = n_tensor // self.nx
        shifts = [(x, y) for y in range(self.ny) for x in range(self.nx)]
        self.shifts = sorted(shifts, key=lambda xy: ((xy[0] > 0) + (xy[1] > 0), xy[1], xy[0]))
        self.along_x = [j for j, (x, y) in enumerate(self.shifts) if x and not y]
        self.along_y = [j for j, (x, y) in enumerate(self.shifts) if y and not x]
        self.far = [j for j, (x, y) in enumerate(self.shifts) if x and y]
        self.cap = min(rows, max(2, 2 * rows // n_dp))
        self.whole = self.cap // 16 * 16
        self.rest = self.cap - self.whole
        self.cols = emb // CHUNKS
        self.tiles = self.cols // 128
        self.folded = -(-self.rest * self.tiles // 16) * 16
        self.block = self.whole * self.tiles + self.folded
        self.slots = n_dp * self.cap
        self.lanes = -(-self.slots // 128) * 128


def kernel(
    z,
    features,
    w_hidden,
    w_embed,
    members,
    hbm_owner,
    hbm_local,
    hbm_cluster,
    hbm_valid,
    best,
    feat,
    w1,
    w2,
    raw,
    doc_owner,
    doc_local,
    member_cluster,
    member_valid,
    unit,
    member_tag,
    sums_out,
    sums_in,
    docs_out,
    docs_in,
    tags_out,
    tags_in,
    answer_out,
    answer_in,
    local_sem,
    feat_send,
    feat_recv,
    unit_send,
    unit_recv,
    mtag_send,
    mtag_recv,
    sums_send,
    sums_recv,
    docs_send,
    docs_recv,
    tags_send,
    tags_recv,
    answer_send,
    answer_recv,
):
    p = lax.axis_index("dp")
    t = lax.axis_index("tensor")
    tx, ty = lax.rem(t, z.nx), lax.div(t, z.nx)
    half = z.hid // 2
    sent = []

    def forward_of(j):
        dx, dy = z.shifts[j]
        return lax.rem(ty + dy, z.ny) * z.nx + lax.rem(tx + dx, z.nx)

    def source_of(j):
        dx, dy = z.shifts[j]
        return lax.rem(ty + z.ny - dy, z.ny) * z.nx + lax.rem(tx + z.nx - dx, z.nx)

    def remote(src, dst, send, recv, **device):
        copy = pltpu.make_async_remote_copy(
            src_ref=src, dst_ref=dst, send_sem=send, recv_sem=recv, device_id=device,
            device_id_type=MESH,
        )
        copy.start()
        sent.append(copy)
        return copy

    barrier = pltpu.get_barrier_semaphore()
    for j in range(1, z.n_tensor):
        pl.semaphore_signal(barrier, inc=1, device_id={"tensor": forward_of(j)}, device_id_type=MESH)
    for k in range(1, z.n_dp):
        pl.semaphore_signal(
            barrier, inc=1, device_id={"dp": lax.rem(p + k, z.n_dp)}, device_id_type=MESH
        )

    own = [
        pltpu.make_async_copy(features.at[:, pl.ds(h * half, half)], feat.at[h, 0], local_sem.at[h])
        for h in (0, 1)
    ]
    load_w1 = [
        pltpu.make_async_copy(
            w_hidden.at[pl.ds(h * half, half)], w1.at[pl.ds(h * half, half)], local_sem.at[2 + h]
        )
        for h in (0, 1)
    ]
    load_w2 = pltpu.make_async_copy(w_embed, w2, local_sem.at[4])
    load_members = pltpu.make_async_copy(members.at[0], raw, local_sem.at[5])
    load_small = [
        pltpu.make_async_copy(src, dst, local_sem.at[6 + i])
        for i, (src, dst) in enumerate(
            (
                (hbm_owner, doc_owner),
                (hbm_local, doc_local),
                (hbm_cluster, member_cluster),
                (hbm_valid, member_valid),
            )
        )
    ]
    for copy in (*load_small, *own, *load_w1, load_w2, load_members):
        copy.start()

    pl.semaphore_wait(barrier, z.n_tensor - 1 + z.n_dp - 1)

    feat_copy = {}

    def send_feature(h, j, src, target):
        feat_copy[h, j] = remote(
            src, feat.at[h, j], feat_send.at[h, j], feat_recv.at[h, j], tensor=forward_of(target)
        )

    along_x, along_y, far = z.along_x, z.along_y, z.far

    def corner(x, y):
        return z.shifts.index((z.shifts[x][0], z.shifts[y][1]))

    for first in (0, 1):
        for j in along_x:
            h = first
            send_feature(h, j, features.at[:, pl.ds(h * half, half)], j)
        for j in along_y:
            h = 1 - first
            send_feature(h, j, features.at[:, pl.ds(h * half, half)], j)

    for copy in load_small:
        copy.wait()
    rows, wide = z.rows, doc_owner.shape[1]
    mine = iota((rows, wide), 1) == iota((rows, wide), 0) + (t * rows).astype(F32)
    owner = jnp.sum(jnp.where(mine, doc_owner[...].astype(F32), 0.0), axis=1, keepdims=True)
    local = jnp.sum(jnp.where(mine, doc_local[...].reshape(1, wide).astype(F32), 0.0), axis=1, keepdims=True)
    step = owner - p.astype(F32)
    step = jnp.where(step < 0.0, step + float(z.n_dp), step)
    step_row = to_row(step, rows)
    same = step == step_row
    above = iota((rows, rows), 0)
    across = iota((rows, rows), 1)
    rank = jnp.sum(jnp.where(same & (across < above), 1.0, 0.0), axis=1, keepdims=True)
    rank_row = jnp.sum(jnp.where(same & (above < across), 1.0, 0.0), axis=0, keepdims=True)
    place = jnp.where(
        rank < float(z.whole),
        step * float(z.whole) + rank,
        float(z.n_dp * z.whole) + step * float(z.rest) + rank - float(z.whole),
    )
    placed = iota((rows, z.lanes), 1) == place
    step_hot = jnp.where(iota((z.n_dp, rows), 0) == step_row, 1.0, 0.0).astype(BF16)
    tags = jnp.dot(
        step_hot,
        jnp.where(placed, local + 1.0, 0.0).astype(BF16),
        preferred_element_type=F32,
    )
    for k in range(z.n_dp):
        tags_out[k] = tags[k : k + 1, :]
    tags_copy = [
        remote(
            tags_out.at[k], tags_in.at[k], tags_send.at[k], tags_recv.at[k],
            dp=lax.rem(p + k, z.n_dp),
        )
        for k in range(1, z.n_dp)
    ]

    member_tag[0] = jnp.where(
        member_valid[...] == 1, member_cluster[...].astype(F32) + 1.0, -1.0
    )
    load_members.wait()
    values = raw[...].astype(F32)
    unit[:, 0] = (
        (values / jnp.sqrt(jnp.sum(values * values, axis=1, keepdims=True) + EPSILON))
        .astype(BF16)
        .reshape(2, z.members // 2, z.emb)
    )
    mtag_copy = [
        remote(
            member_tag.at[0], member_tag.at[j], mtag_send.at[j], mtag_recv.at[j],
            tensor=forward_of(j),
        )
        for j in range(1, z.n_tensor)
    ]

    def head(first, last):
        count = last - first
        total = jnp.dot(
            feat[0, first:last].reshape(count * z.rows, half),
            w1[:half, :],
            preferred_element_type=F32,
        )
        total += jnp.dot(
            feat[1, first:last].reshape(count * z.rows, half),
            w1[half:, :],
            preferred_element_type=F32,
        )
        return jax.nn.gelu(total).astype(BF16)

    def embed(hidden, c, first, last):
        sums_out[c, first:last] = (
            jnp.dot(hidden, w2[:, c * z.cols : (c + 1) * z.cols], preferred_element_type=F32)
            .astype(BF16)
            .reshape(last - first, z.rows, z.cols)
        )

    def send_sums(c, first, last):
        for j in range(first, last):
            sums_copy[c, j] = remote(
                sums_out.at[c, j], sums_in.at[c, j], sums_send.at[c, j], sums_recv.at[c, j],
                tensor=source_of(j),
            )

    sums_copy = {}
    for j in along_x:
        feat_copy[0, j].wait_recv()
        for y in along_y:
            send_feature(0, corner(j, y), feat.at[0, j], y)
    for j in along_y:
        feat_copy[1, j].wait_recv()
        for x in along_x:
            send_feature(1, corner(x, j), feat.at[1, j], x)
    for copy in (*own, *load_w1, load_w2):
        copy.wait()
    hidden = head(0, 1)
    for c in range(CHUNKS):
        embed(hidden, c, 0, 1)

    near = 1 + len(along_x) + len(along_y)
    for j in along_x:
        feat_copy[1, j].wait_recv()
    for j in along_y:
        feat_copy[0, j].wait_recv()
    if near > 1:
        hidden = head(1, near)
        for c in range(CHUNKS):
            embed(hidden, c, 1, near)
    for j in far:
        feat_copy[0, j].wait_recv()
        feat_copy[1, j].wait_recv()
    send_sums(0, 1, near)
    if far:
        hidden = head(near, z.n_tensor)
    for c in range(CHUNKS):
        if c:
            send_sums(c, 1, near)
        if far:
            embed(hidden, c, near, z.n_tensor)
            send_sums(c, near, z.n_tensor)

    unit_copy = {}

    def send_unit(h, j, held, target):
        unit_copy[h, j] = remote(
            unit.at[h, held], unit.at[h, j], unit_send.at[h, j], unit_recv.at[h, j],
            tensor=forward_of(target),
        )

    code = step_row * float(z.cap) + rank_row
    code = code.reshape(1, 1, rows)
    if z.whole:
        shape = (z.n_dp, z.whole, rows)
        pack_whole = jnp.where(
            code == iota(shape, 0) * float(z.cap) + iota(shape, 1), 1.0, 0.0
        ).reshape(z.n_dp * z.whole, rows).astype(BF16)
    pack_rest = []
    if z.rest:
        shape = (z.n_dp, z.folded, rows)
        for c in range(z.tiles):
            at = iota(shape, 1) - float(c * z.rest)
            inside = (at >= 0.0) & (at < float(z.rest))
            hit = inside & (code == iota(shape, 0) * float(z.cap) + float(z.whole) + at)
            pack_rest.append(
                jnp.where(hit, 1.0, 0.0).reshape(z.n_dp * z.folded, rows).astype(BF16)
            )

    square = jnp.zeros((rows, 1), F32)
    docs_copy = {}
    for c in range(CHUNKS):
        proj = sums_out[c, 0].astype(F32)
        for j in range(1, z.n_tensor):
            sums_copy[c, j].wait_recv()
            proj += sums_in[c, j].astype(F32)
        query = proj.astype(BF16)
        if z.whole:
            packed = jnp.dot(pack_whole, query, preferred_element_type=F32).astype(BF16)
        if z.rest:
            tail = jnp.zeros((z.n_dp * z.folded, 128), F32)
            for i in range(z.tiles):
                tail += jnp.dot(
                    pack_rest[i], query[:, i * 128 : (i + 1) * 128], preferred_element_type=F32
                )
            tail = tail.astype(BF16)
        for k in [*range(1, z.n_dp), 0]:
            target = docs_out if k else docs_in
            if z.whole:
                for i in range(z.tiles):
                    target[c, k, i * z.whole : (i + 1) * z.whole, :] = packed[
                        k * z.whole : (k + 1) * z.whole, i * 128 : (i + 1) * 128
                    ]
            if z.rest:
                target[c, k, z.tiles * z.whole :, :] = tail[k * z.folded : (k + 1) * z.folded, :]
            if k:
                docs_copy[c, k] = remote(
                    docs_out.at[c, k], docs_in.at[c, k], docs_send.at[c, k], docs_recv.at[c, k],
                    dp=lax.rem(p + k, z.n_dp),
                )
        square += jnp.sum(proj * proj, axis=1, keepdims=True)
        if c == 0:
            for first in (0, 1):
                for j in along_x:
                    send_unit(first, j, 0, j)
                for j in along_y:
                    send_unit(1 - first, j, 0, j)
    inverse = 1.0 / jnp.sqrt(square + EPSILON)
    for j in along_x:
        unit_copy[0, j].wait_recv()
        for y in along_y:
            send_unit(0, corner(j, y), j, y)
    for j in along_y:
        unit_copy[1, j].wait_recv()
        for x in along_x:
            send_unit(1, corner(x, j), j, x)

    tag_row = tags_out[0]
    for k in range(1, z.n_dp):
        tags_copy[k - 1].wait_recv()
        tag_row += tags_in[k]
    tag_row = tag_row[:, : z.slots]
    for copy in mtag_copy:
        copy.wait_recv()
    allowed = [to_column(member_tag[j], z.members) for j in range(z.n_tensor)]

    unfold = []
    if z.rest:
        shape = (z.n_dp * z.rest, z.n_dp * z.folded)
        out_row, in_row = iota(shape, 0), iota(shape, 1)
        for i in range(z.tiles):
            hit = jnp.zeros(shape, F32)
            for k in range(z.n_dp):
                at = out_row - float(k * z.rest)
                inside = (at >= 0.0) & (at < float(z.rest))
                hit = jnp.where(
                    inside & (in_row == at + float(k * z.folded + i * z.rest)), 1.0, hit
                )
            unfold.append(hit.astype(BF16))

    arrived = []
    for c in range(CHUNKS):
        for k in range(1, z.n_dp):
            docs_copy[c, k].wait_recv()
        parts = []
        if z.whole:
            parts.append(
                jnp.concatenate(
                    [
                        docs_in[c, :, i * z.whole : (i + 1) * z.whole, :].reshape(
                            z.n_dp * z.whole, 128
                        )
                        for i in range(z.tiles)
                    ],
                    axis=1,
                )
            )
        if z.rest:
            tail = docs_in[c, :, z.tiles * z.whole :, :].reshape(z.n_dp * z.folded, 128)
            parts.append(
                jnp.concatenate(
                    [
                        jnp.dot(unfold[i], tail, preferred_element_type=F32).astype(BF16)
                        for i in range(z.tiles)
                    ],
                    axis=1,
                )
            )
        arrived.append(jnp.concatenate(parts, axis=0) if len(parts) > 1 else parts[0])
    top = jnp.full((1, z.slots), LOWEST, F32)
    for j in range(z.n_tensor):
        if j in along_x:
            unit_copy[1, j].wait_recv()
        elif j in along_y:
            unit_copy[0, j].wait_recv()
        elif j:
            unit_copy[0, j].wait_recv()
            unit_copy[1, j].wait_recv()
        scores = jnp.zeros((z.members, z.slots), F32)
        for c in range(CHUNKS):
            scores += lax.dot_general(
                unit[:, j, :, c * z.cols : (c + 1) * z.cols].reshape(z.members, z.cols),
                arrived[c],
                (((1,), (1,)), ((), ())),
                preferred_element_type=F32,
            )
        kept = jnp.where(allowed[j] == tag_row, scores, LOWEST)
        top = jnp.maximum(top, jnp.max(kept, axis=0, keepdims=True))
    answer_out[...] = jnp.zeros_like(answer_out)
    answer_out[:, : z.slots] = top

    answer_copy = [
        remote(
            answer_out, answer_in.at[k], answer_send.at[k], answer_recv.at[k],
            dp=lax.rem(p + z.n_dp - k, z.n_dp),
        )
        for k in range(1, z.n_dp)
    ]
    found = jnp.where(step == 0.0, answer_out[...], 0.0)
    for k in range(1, z.n_dp):
        answer_copy[k - 1].wait_recv()
        found = jnp.where(step == float(k), answer_in[k], found)
    value = jnp.sum(jnp.where(placed, found, 0.0), axis=1, keepdims=True)
    best[...] = to_row(jnp.maximum(value * inverse, -1.0), rows)
    for copy in sent:
        copy.wait_send()


def body(features, w_hidden, w_embed, members, doc_owner, doc_local, member_cluster, member_valid):
    n_dp, n_tensor = lax.axis_size("dp"), lax.axis_size("tensor")
    rows, hid = features.shape
    width, emb = w_embed.shape
    z = Sizes(n_dp, n_tensor, rows, hid, width, emb, members.shape[1])
    half = hid // 2
    dma = pltpu.SemaphoreType.DMA
    hbm = pl.BlockSpec(memory_space=pl.ANY)
    vmem = pl.BlockSpec(memory_space=pltpu.VMEM)
    out = pl.pallas_call(
        functools.partial(kernel, z),
        out_shape=pltpu.VMEM((1, rows), F32),
        in_specs=[hbm] * 8,
        out_specs=vmem,
        scratch_shapes=[
            pltpu.VMEM((2, n_tensor, rows, half), BF16),
            pltpu.VMEM((hid, width), BF16),
            pltpu.VMEM((width, emb), BF16),
            pltpu.VMEM((z.members, emb), BF16),
            pltpu.VMEM((1, doc_owner.shape[0]), jnp.int32),
            pltpu.VMEM(doc_local.shape, jnp.int32),
            pltpu.VMEM((1, z.members), jnp.int32),
            pltpu.VMEM((1, z.members), jnp.int32),
            pltpu.VMEM((2, n_tensor, z.members // 2, emb), BF16),
            pltpu.VMEM((n_tensor, 1, z.members), F32),
            pltpu.VMEM((CHUNKS, n_tensor, rows, z.cols), BF16),
            pltpu.VMEM((CHUNKS, n_tensor, rows, z.cols), BF16),
            pltpu.VMEM((CHUNKS, n_dp, z.block, 128), BF16),
            pltpu.VMEM((CHUNKS, n_dp, z.block, 128), BF16),
            pltpu.VMEM((n_dp, 1, z.lanes), F32),
            pltpu.VMEM((n_dp, 1, z.lanes), F32),
            pltpu.VMEM((1, z.lanes), F32),
            pltpu.VMEM((n_dp, 1, z.lanes), F32),
            dma((10,)),
            dma((2, n_tensor)),
            dma((2, n_tensor)),
            dma((2, n_tensor)),
            dma((2, n_tensor)),
            dma((n_tensor,)),
            dma((n_tensor,)),
            dma((CHUNKS, n_tensor)),
            dma((CHUNKS, n_tensor)),
            dma((CHUNKS, n_dp)),
            dma((CHUNKS, n_dp)),
            dma((n_dp,)),
            dma((n_dp,)),
            dma((n_dp,)),
            dma((n_dp,)),
        ],
        compiler_params=pltpu.CompilerParams(
            collective_id=0, has_side_effects=True, vmem_limit_bytes=62 * 1024 * 1024
        ),
        name="match",
    )(
        features,
        w_hidden,
        w_embed,
        members,
        doc_owner.reshape(1, -1),
        doc_local,
        member_cluster,
        member_valid,
    )
    return out.reshape(rows)


def solution(mesh):
    return jax.shard_map(
        body,
        mesh=mesh,
        in_specs=(
            P(("dp", "tensor"), None),
            P(None, "tensor"),
            P("tensor", None),
            P("dp", "tensor", None),
            P("dp", None),
            P("dp"),
            P("dp", "tensor"),
            P("dp", "tensor"),
        ),
        out_specs=P(("dp", "tensor")),
        check_vma=False,
    )
```

```python
import functools
import math

import jax
import jax.numpy as jnp
from jax import lax
from jax.experimental import pallas as pl
from jax.experimental.pallas import tpu as pltpu
from jax.sharding import PartitionSpec as P

EPSILON = 1e-06
MESH = pl.DeviceIdType.MESH
F32 = jnp.float32
BF16 = jnp.bfloat16
LOWEST = -1e30
CHUNKS = 2


def iota(shape, dim):
    return lax.broadcasted_iota(jnp.int32, shape, dim).astype(F32)


def to_column(row, size):
    eye = iota((size, size), 0) == iota((size, size), 1)
    return jnp.sum(jnp.where(eye, row, 0.0), axis=1, keepdims=True)


def to_row(column, size):
    eye = iota((size, size), 0) == iota((size, size), 1)
    return jnp.sum(jnp.where(eye, column, 0.0), axis=0, keepdims=True)


class Sizes:
    def __init__(self, n_dp, n_tensor, rows, hid, width, emb, members):
        self.n_dp, self.n_tensor = n_dp, n_tensor
        self.rows, self.hid, self.width, self.emb, self.members = rows, hid, width, emb, members
        self.nx = max(d for d in range(1, math.isqrt(n_tensor) + 1) if n_tensor % d == 0)
        self.ny = n_tensor // self.nx
        shifts = [(x, y) for y in range(self.ny) for x in range(self.nx)]
        self.shifts = sorted(shifts, key=lambda xy: ((xy[0] > 0) + (xy[1] > 0), xy[1], xy[0]))
        self.along_x = [j for j, (x, y) in enumerate(self.shifts) if x and not y]
        self.along_y = [j for j, (x, y) in enumerate(self.shifts) if y and not x]
        self.far = [j for j, (x, y) in enumerate(self.shifts) if x and y]
        self.cap = min(rows, max(2, 2 * rows // n_dp))
        self.whole = self.cap // 16 * 16
        self.rest = self.cap - self.whole
        self.cols = emb // CHUNKS
        self.tiles = self.cols // 128
        self.folded = -(-self.rest * self.tiles // 16) * 16
        self.block = self.whole * self.tiles + self.folded
        self.slots = n_dp * self.cap
        self.lanes = -(-self.slots // 128) * 128


def kernel(
    z,
    features,
    w_hidden,
    w_embed,
    members,
    hbm_owner,
    hbm_local,
    hbm_cluster,
    hbm_valid,
    best,
    feat,
    w1,
    w2,
    raw,
    doc_owner,
    doc_local,
    member_cluster,
    member_valid,
    unit,
    member_tag,
    sums_out,
    sums_in,
    docs_out,
    docs_in,
    tags_out,
    tags_in,
    answer_out,
    answer_in,
    local_sem,
    feat_send,
    feat_recv,
    unit_send,
    unit_recv,
    mtag_send,
    mtag_recv,
    sums_send,
    sums_recv,
    docs_send,
    docs_recv,
    tags_send,
    tags_recv,
    answer_send,
    answer_recv,
):
    p = lax.axis_index("dp")
    t = lax.axis_index("tensor")
    tx, ty = lax.rem(t, z.nx), lax.div(t, z.nx)
    half = z.hid // 2
    sent = []

    def forward_of(j):
        dx, dy = z.shifts[j]
        return lax.rem(ty + dy, z.ny) * z.nx + lax.rem(tx + dx, z.nx)

    def source_of(j):
        dx, dy = z.shifts[j]
        return lax.rem(ty + z.ny - dy, z.ny) * z.nx + lax.rem(tx + z.nx - dx, z.nx)

    def remote(src, dst, send, recv, **device):
        copy = pltpu.make_async_remote_copy(
            src_ref=src, dst_ref=dst, send_sem=send, recv_sem=recv, device_id=device,
            device_id_type=MESH,
        )
        copy.start()
        sent.append(copy)
        return copy

    barrier = pltpu.get_barrier_semaphore()
    for j in range(1, z.n_tensor):
        pl.semaphore_signal(barrier, inc=1, device_id={"tensor": forward_of(j)}, device_id_type=MESH)
    for k in range(1, z.n_dp):
        pl.semaphore_signal(
            barrier, inc=1, device_id={"dp": lax.rem(p + k, z.n_dp)}, device_id_type=MESH
        )

    own = [
        pltpu.make_async_copy(features.at[:, pl.ds(h * half, half)], feat.at[h, 0], local_sem.at[h])
        for h in (0, 1)
    ]
    load_w1 = [
        pltpu.make_async_copy(
            w_hidden.at[pl.ds(h * half, half)], w1.at[pl.ds(h * half, half)], local_sem.at[2 + h]
        )
        for h in (0, 1)
    ]
    load_w2 = pltpu.make_async_copy(w_embed, w2, local_sem.at[4])
    load_members = pltpu.make_async_copy(members.at[0], raw, local_sem.at[5])
    load_small = [
        pltpu.make_async_copy(src, dst, local_sem.at[6 + i])
        for i, (src, dst) in enumerate(
            (
                (hbm_owner, doc_owner),
                (hbm_local, doc_local),
                (hbm_cluster, member_cluster),
                (hbm_valid, member_valid),
            )
        )
    ]
    for copy in (*load_small, *own, *load_w1, load_w2, load_members):
        copy.start()

    pl.semaphore_wait(barrier, z.n_tensor - 1 + z.n_dp - 1)

    feat_copy = {}

    def send_feature(h, j, src, target):
        feat_copy[h, j] = remote(
            src, feat.at[h, j], feat_send.at[h, j], feat_recv.at[h, j], tensor=forward_of(target)
        )

    along_x, along_y, far = z.along_x, z.along_y, z.far

    def corner(x, y):
        return z.shifts.index((z.shifts[x][0], z.shifts[y][1]))

    def send_own_features(first):
        for j in along_x:
            send_feature(first, j, features.at[:, pl.ds(first * half, half)], j)
        for j in along_y:
            send_feature(1 - first, j, features.at[:, pl.ds((1 - first) * half, half)], j)

    send_own_features(0)

    for copy in load_small:
        copy.wait()
    rows, wide = z.rows, doc_owner.shape[1]
    mine = iota((rows, wide), 1) == iota((rows, wide), 0) + (t * rows).astype(F32)
    owner = jnp.sum(jnp.where(mine, doc_owner[...].astype(F32), 0.0), axis=1, keepdims=True)
    local = jnp.sum(jnp.where(mine, doc_local[...].reshape(1, wide).astype(F32), 0.0), axis=1, keepdims=True)
    step = owner - p.astype(F32)
    step = jnp.where(step < 0.0, step + float(z.n_dp), step)
    step_row = to_row(step, rows)
    same = step == step_row
    above = iota((rows, rows), 0)
    across = iota((rows, rows), 1)
    rank = jnp.sum(jnp.where(same & (across < above), 1.0, 0.0), axis=1, keepdims=True)
    rank_row = jnp.sum(jnp.where(same & (above < across), 1.0, 0.0), axis=0, keepdims=True)
    place = jnp.where(
        rank < float(z.whole),
        step * float(z.whole) + rank,
        float(z.n_dp * z.whole) + step * float(z.rest) + rank - float(z.whole),
    )
    placed = iota((rows, z.lanes), 1) == place
    step_hot = jnp.where(iota((z.n_dp, rows), 0) == step_row, 1.0, 0.0).astype(BF16)
    tags = jnp.dot(
        step_hot,
        jnp.where(placed, local + 1.0, 0.0).astype(BF16),
        preferred_element_type=F32,
    )
    for k in range(z.n_dp):
        tags_out[k] = tags[k : k + 1, :]
    tags_copy = [
        remote(
            tags_out.at[k], tags_in.at[k], tags_send.at[k], tags_recv.at[k],
            dp=lax.rem(p + k, z.n_dp),
        )
        for k in range(1, z.n_dp)
    ]

    member_tag[0] = jnp.where(
        member_valid[...] == 1, member_cluster[...].astype(F32) + 1.0, -1.0
    )
    load_members.wait()
    values = raw[...].astype(F32)
    unit[:, 0] = (
        (values / jnp.sqrt(jnp.sum(values * values, axis=1, keepdims=True) + EPSILON))
        .astype(BF16)
        .reshape(2, z.members // 2, z.emb)
    )
    mtag_copy = [
        remote(
            member_tag.at[0], member_tag.at[j], mtag_send.at[j], mtag_recv.at[j],
            tensor=forward_of(j),
        )
        for j in range(1, z.n_tensor)
    ]

    def head(first, last):
        count = last - first
        total = jnp.dot(
            feat[0, first:last].reshape(count * z.rows, half),
            w1[:half, :],
            preferred_element_type=F32,
        )
        total += jnp.dot(
            feat[1, first:last].reshape(count * z.rows, half),
            w1[half:, :],
            preferred_element_type=F32,
        )
        return jax.nn.gelu(total).astype(BF16)

    def embed(hidden, c, first, last):
        sums_out[c, first:last] = (
            jnp.dot(hidden, w2[:, c * z.cols : (c + 1) * z.cols], preferred_element_type=F32)
            .astype(BF16)
            .reshape(last - first, z.rows, z.cols)
        )

    def send_sums(c, first, last):
        for j in range(first, last):
            sums_copy[c, j] = remote(
                sums_out.at[c, j], sums_in.at[c, j], sums_send.at[c, j], sums_recv.at[c, j],
                tensor=source_of(j),
            )

    sums_copy = {}
    send_own_features(1)
    for j in along_x:
        feat_copy[0, j].wait_recv()
        for y in along_y:
            send_feature(0, corner(j, y), feat.at[0, j], y)
    for j in along_y:
        feat_copy[1, j].wait_recv()
        for x in along_x:
            send_feature(1, corner(x, j), feat.at[1, j], x)
    for copy in (*own, *load_w1, load_w2):
        copy.wait()
    hidden = head(0, 1)
    for c in range(CHUNKS):
        embed(hidden, c, 0, 1)

    near = 1 + len(along_x) + len(along_y)
    for j in along_x:
        feat_copy[1, j].wait_recv()
    for j in along_y:
        feat_copy[0, j].wait_recv()
    if near > 1:
        hidden = head(1, near)
        for c in range(CHUNKS):
            embed(hidden, c, 1, near)
    for j in far:
        feat_copy[0, j].wait_recv()
        feat_copy[1, j].wait_recv()
    send_sums(0, 1, near)
    if far:
        hidden = head(near, z.n_tensor)
    for c in range(CHUNKS):
        if c:
            send_sums(c, 1, near)
        if far:
            embed(hidden, c, near, z.n_tensor)
            send_sums(c, near, z.n_tensor)

    unit_copy = {}

    def send_unit(h, j, held, target):
        unit_copy[h, j] = remote(
            unit.at[h, held], unit.at[h, j], unit_send.at[h, j], unit_recv.at[h, j],
            tensor=forward_of(target),
        )

    code = step_row * float(z.cap) + rank_row
    code = code.reshape(1, 1, rows)
    if z.whole:
        shape = (z.n_dp, z.whole, rows)
        pack_whole = jnp.where(
            code == iota(shape, 0) * float(z.cap) + iota(shape, 1), 1.0, 0.0
        ).reshape(z.n_dp * z.whole, rows).astype(BF16)
    pack_rest = []
    if z.rest:
        shape = (z.n_dp, z.folded, rows)
        for c in range(z.tiles):
            at = iota(shape, 1) - float(c * z.rest)
            inside = (at >= 0.0) & (at < float(z.rest))
            hit = inside & (code == iota(shape, 0) * float(z.cap) + float(z.whole) + at)
            pack_rest.append(
                jnp.where(hit, 1.0, 0.0).reshape(z.n_dp * z.folded, rows).astype(BF16)
            )

    def send_own_units(first):
        for j in along_x:
            send_unit(first, j, 0, j)
        for j in along_y:
            send_unit(1 - first, j, 0, j)

    square = jnp.zeros((rows, 1), F32)
    docs_copy = {}
    for c in range(CHUNKS):
        proj = sums_out[c, 0].astype(F32)
        for j in range(1, z.n_tensor):
            sums_copy[c, j].wait_recv()
            proj += sums_in[c, j].astype(F32)
        query = proj.astype(BF16)
        if z.whole:
            packed = jnp.dot(pack_whole, query, preferred_element_type=F32).astype(BF16)
        if z.rest:
            tail = jnp.zeros((z.n_dp * z.folded, 128), F32)
            for i in range(z.tiles):
                tail += jnp.dot(
                    pack_rest[i], query[:, i * 128 : (i + 1) * 128], preferred_element_type=F32
                )
            tail = tail.astype(BF16)
        for k in [*range(1, z.n_dp), 0]:
            target = docs_out if k else docs_in
            if z.whole:
                for i in range(z.tiles):
                    target[c, k, i * z.whole : (i + 1) * z.whole, :] = packed[
                        k * z.whole : (k + 1) * z.whole, i * 128 : (i + 1) * 128
                    ]
            if z.rest:
                target[c, k, z.tiles * z.whole :, :] = tail[k * z.folded : (k + 1) * z.folded, :]
            if k:
                docs_copy[c, k] = remote(
                    docs_out.at[c, k], docs_in.at[c, k], docs_send.at[c, k], docs_recv.at[c, k],
                    dp=lax.rem(p + k, z.n_dp),
                )
        square += jnp.sum(proj * proj, axis=1, keepdims=True)
        if c == 0:
            send_own_units(0)
    send_own_units(1)
    inverse = 1.0 / jnp.sqrt(square + EPSILON)
    for j in along_x:
        unit_copy[0, j].wait_recv()
        for y in along_y:
            send_unit(0, corner(j, y), j, y)
    for j in along_y:
        unit_copy[1, j].wait_recv()
        for x in along_x:
            send_unit(1, corner(x, j), j, x)

    tag_row = tags_out[0]
    for k in range(1, z.n_dp):
        tags_copy[k - 1].wait_recv()
        tag_row += tags_in[k]
    tag_row = tag_row[:, : z.slots]
    for copy in mtag_copy:
        copy.wait_recv()
    allowed = [to_column(member_tag[j], z.members) for j in range(z.n_tensor)]

    unfold = []
    if z.rest:
        shape = (z.n_dp * z.rest, z.n_dp * z.folded)
        out_row, in_row = iota(shape, 0), iota(shape, 1)
        for i in range(z.tiles):
            hit = jnp.zeros(shape, F32)
            for k in range(z.n_dp):
                at = out_row - float(k * z.rest)
                inside = (at >= 0.0) & (at < float(z.rest))
                hit = jnp.where(
                    inside & (in_row == at + float(k * z.folded + i * z.rest)), 1.0, hit
                )
            unfold.append(hit.astype(BF16))

    arrived = []
    for c in range(CHUNKS):
        for k in range(1, z.n_dp):
            docs_copy[c, k].wait_recv()
        parts = []
        if z.whole:
            parts.append(
                jnp.concatenate(
                    [
                        docs_in[c, :, i * z.whole : (i + 1) * z.whole, :].reshape(
                            z.n_dp * z.whole, 128
                        )
                        for i in range(z.tiles)
                    ],
                    axis=1,
                )
            )
        if z.rest:
            tail = docs_in[c, :, z.tiles * z.whole :, :].reshape(z.n_dp * z.folded, 128)
            parts.append(
                jnp.concatenate(
                    [
                        jnp.dot(unfold[i], tail, preferred_element_type=F32).astype(BF16)
                        for i in range(z.tiles)
                    ],
                    axis=1,
                )
            )
        arrived.append(jnp.concatenate(parts, axis=0) if len(parts) > 1 else parts[0])
    top = jnp.full((1, z.slots), LOWEST, F32)
    for j in range(z.n_tensor):
        if j in along_x:
            unit_copy[1, j].wait_recv()
        elif j in along_y:
            unit_copy[0, j].wait_recv()
        elif j:
            unit_copy[0, j].wait_recv()
            unit_copy[1, j].wait_recv()
        scores = jnp.zeros((z.members, z.slots), F32)
        for c in range(CHUNKS):
            scores += lax.dot_general(
                unit[:, j, :, c * z.cols : (c + 1) * z.cols].reshape(z.members, z.cols),
                arrived[c],
                (((1,), (1,)), ((), ())),
                preferred_element_type=F32,
            )
        kept = jnp.where(allowed[j] == tag_row, scores, LOWEST)
        top = jnp.maximum(top, jnp.max(kept, axis=0, keepdims=True))
    answer_out[...] = jnp.zeros_like(answer_out)
    answer_out[:, : z.slots] = top

    answer_copy = [
        remote(
            answer_out, answer_in.at[k], answer_send.at[k], answer_recv.at[k],
            dp=lax.rem(p + z.n_dp - k, z.n_dp),
        )
        for k in range(1, z.n_dp)
    ]
    found = jnp.where(step == 0.0, answer_out[...], 0.0)
    for k in range(1, z.n_dp):
        answer_copy[k - 1].wait_recv()
        found = jnp.where(step == float(k), answer_in[k], found)
    value = jnp.sum(jnp.where(placed, found, 0.0), axis=1, keepdims=True)
    best[...] = to_row(jnp.maximum(value * inverse, -1.0), rows)
    for copy in sent:
        copy.wait_send()


def body(features, w_hidden, w_embed, members, doc_owner, doc_local, member_cluster, member_valid):
    n_dp, n_tensor = lax.axis_size("dp"), lax.axis_size("tensor")
    rows, hid = features.shape
    width, emb = w_embed.shape
    z = Sizes(n_dp, n_tensor, rows, hid, width, emb, members.shape[1])
    half = hid // 2
    dma = pltpu.SemaphoreType.DMA
    hbm = pl.BlockSpec(memory_space=pl.ANY)
    vmem = pl.BlockSpec(memory_space=pltpu.VMEM)
    out = pl.pallas_call(
        functools.partial(kernel, z),
        out_shape=pltpu.VMEM((1, rows), F32),
        in_specs=[hbm] * 8,
        out_specs=vmem,
        scratch_shapes=[
            pltpu.VMEM((2, n_tensor, rows, half), BF16),
            pltpu.VMEM((hid, width), BF16),
            pltpu.VMEM((width, emb), BF16),
            pltpu.VMEM((z.members, emb), BF16),
            pltpu.VMEM((1, doc_owner.shape[0]), jnp.int32),
            pltpu.VMEM(doc_local.shape, jnp.int32),
            pltpu.VMEM((1, z.members), jnp.int32),
            pltpu.VMEM((1, z.members), jnp.int32),
            pltpu.VMEM((2, n_tensor, z.members // 2, emb), BF16),
            pltpu.VMEM((n_tensor, 1, z.members), F32),
            pltpu.VMEM((CHUNKS, n_tensor, rows, z.cols), BF16),
            pltpu.VMEM((CHUNKS, n_tensor, rows, z.cols), BF16),
            pltpu.VMEM((CHUNKS, n_dp, z.block, 128), BF16),
            pltpu.VMEM((CHUNKS, n_dp, z.block, 128), BF16),
            pltpu.VMEM((n_dp, 1, z.lanes), F32),
            pltpu.VMEM((n_dp, 1, z.lanes), F32),
            pltpu.VMEM((1, z.lanes), F32),
            pltpu.VMEM((n_dp, 1, z.lanes), F32),
            dma((10,)),
            dma((2, n_tensor)),
            dma((2, n_tensor)),
            dma((2, n_tensor)),
            dma((2, n_tensor)),
            dma((n_tensor,)),
            dma((n_tensor,)),
            dma((CHUNKS, n_tensor)),
            dma((CHUNKS, n_tensor)),
            dma((CHUNKS, n_dp)),
            dma((CHUNKS, n_dp)),
            dma((n_dp,)),
            dma((n_dp,)),
            dma((n_dp,)),
            dma((n_dp,)),
        ],
        compiler_params=pltpu.CompilerParams(
            collective_id=0, has_side_effects=True, vmem_limit_bytes=62 * 1024 * 1024
        ),
        name="match",
    )(
        features,
        w_hidden,
        w_embed,
        members,
        doc_owner.reshape(1, -1),
        doc_local,
        member_cluster,
        member_valid,
    )
    return out.reshape(rows)


def solution(mesh):
    return jax.shard_map(
        body,
        mesh=mesh,
        in_specs=(
            P(("dp", "tensor"), None),
            P(None, "tensor"),
            P("tensor", None),
            P("dp", "tensor", None),
            P("dp", None),
            P("dp"),
            P("dp", "tensor"),
            P("dp", "tensor"),
        ),
        out_specs=P(("dp", "tensor")),
        check_vma=False,
    )
```

```python
import functools
import math

import jax
import jax.numpy as jnp
from jax import lax
from jax.experimental import pallas as pl
from jax.experimental.pallas import tpu as pltpu
from jax.sharding import PartitionSpec as P

EPSILON = 1e-06
MESH = pl.DeviceIdType.MESH
F32 = jnp.float32
BF16 = jnp.bfloat16
LOWEST = -1e30
CHUNKS = 2


def iota(shape, dim):
    return lax.broadcasted_iota(jnp.int32, shape, dim).astype(F32)


def to_column(row, size):
    eye = iota((size, size), 0) == iota((size, size), 1)
    return jnp.sum(jnp.where(eye, row, 0.0), axis=1, keepdims=True)


def to_row(column, size):
    eye = iota((size, size), 0) == iota((size, size), 1)
    return jnp.sum(jnp.where(eye, column, 0.0), axis=0, keepdims=True)


class Sizes:
    def __init__(self, n_dp, n_tensor, rows, hid, width, emb, members):
        self.n_dp, self.n_tensor = n_dp, n_tensor
        self.rows, self.hid, self.width, self.emb, self.members = rows, hid, width, emb, members
        self.nx = max(d for d in range(1, math.isqrt(n_tensor) + 1) if n_tensor % d == 0)
        self.ny = n_tensor // self.nx
        shifts = [(x, y) for y in range(self.ny) for x in range(self.nx)]
        self.shifts = sorted(shifts, key=lambda xy: ((xy[0] > 0) + (xy[1] > 0), xy[1], xy[0]))
        self.along_x = [j for j, (x, y) in enumerate(self.shifts) if x and not y]
        self.along_y = [j for j, (x, y) in enumerate(self.shifts) if y and not x]
        self.far = [j for j, (x, y) in enumerate(self.shifts) if x and y]
        self.cap = min(rows, max(2, 2 * rows // n_dp))
        self.whole = self.cap // 16 * 16
        self.rest = self.cap - self.whole
        self.cols = emb // CHUNKS
        self.tiles = self.cols // 128
        self.folded = -(-self.rest * self.tiles // 16) * 16
        self.block = self.whole * self.tiles + self.folded
        self.slots = n_dp * self.cap
        self.lanes = -(-self.slots // 128) * 128


def kernel(
    z,
    features,
    w_hidden,
    w_embed,
    members,
    hbm_owner,
    hbm_local,
    hbm_cluster,
    hbm_valid,
    best,
    feat,
    w1,
    w2,
    raw,
    doc_owner,
    doc_local,
    member_cluster,
    member_valid,
    unit,
    member_tag,
    sums_out,
    sums_in,
    docs_out,
    docs_in,
    tags_out,
    tags_in,
    answer_out,
    answer_in,
    local_sem,
    feat_send,
    feat_recv,
    unit_send,
    unit_recv,
    mtag_send,
    mtag_recv,
    sums_send,
    sums_recv,
    docs_send,
    docs_recv,
    tags_send,
    tags_recv,
    answer_send,
    answer_recv,
):
    p = lax.axis_index("dp")
    t = lax.axis_index("tensor")
    tx, ty = lax.rem(t, z.nx), lax.div(t, z.nx)
    half = z.hid // 2
    sent = []

    def forward_of(j):
        dx, dy = z.shifts[j]
        return lax.rem(ty + dy, z.ny) * z.nx + lax.rem(tx + dx, z.nx)

    def source_of(j):
        dx, dy = z.shifts[j]
        return lax.rem(ty + z.ny - dy, z.ny) * z.nx + lax.rem(tx + z.nx - dx, z.nx)

    def remote(src, dst, send, recv, **device):
        copy = pltpu.make_async_remote_copy(
            src_ref=src, dst_ref=dst, send_sem=send, recv_sem=recv, device_id=device,
            device_id_type=MESH,
        )
        copy.start()
        sent.append(copy)
        return copy

    barrier = pltpu.get_barrier_semaphore()
    for j in range(1, z.n_tensor):
        pl.semaphore_signal(barrier, inc=1, device_id={"tensor": forward_of(j)}, device_id_type=MESH)
    for k in range(1, z.n_dp):
        pl.semaphore_signal(
            barrier, inc=1, device_id={"dp": lax.rem(p + k, z.n_dp)}, device_id_type=MESH
        )

    own = [
        pltpu.make_async_copy(features.at[:, pl.ds(h * half, half)], feat.at[h, 0], local_sem.at[h])
        for h in (0, 1)
    ]
    load_w1 = [
        pltpu.make_async_copy(
            w_hidden.at[pl.ds(h * half, half)], w1.at[pl.ds(h * half, half)], local_sem.at[2 + h]
        )
        for h in (0, 1)
    ]
    load_w2 = pltpu.make_async_copy(w_embed, w2, local_sem.at[4])
    load_members = pltpu.make_async_copy(members.at[0], raw, local_sem.at[5])
    load_small = [
        pltpu.make_async_copy(src, dst, local_sem.at[6 + i])
        for i, (src, dst) in enumerate(
            (
                (hbm_owner, doc_owner),
                (hbm_local, doc_local),
                (hbm_cluster, member_cluster),
                (hbm_valid, member_valid),
            )
        )
    ]
    for copy in (*load_small, *own, *load_w1, load_w2, load_members):
        copy.start()

    pl.semaphore_wait(barrier, z.n_tensor - 1 + z.n_dp - 1)

    feat_copy = {}

    def send_feature(h, j, src, target):
        feat_copy[h, j] = remote(
            src, feat.at[h, j], feat_send.at[h, j], feat_recv.at[h, j], tensor=forward_of(target)
        )

    along_x, along_y, far = z.along_x, z.along_y, z.far

    def corner(x, y):
        return z.shifts.index((z.shifts[x][0], z.shifts[y][1]))

    def send_own_features(first):
        for j in along_x:
            send_feature(first, j, features.at[:, pl.ds(first * half, half)], j)
        for j in along_y:
            send_feature(1 - first, j, features.at[:, pl.ds((1 - first) * half, half)], j)

    send_own_features(0)

    for copy in load_small:
        copy.wait()
    rows, wide = z.rows, doc_owner.shape[1]
    mine = iota((rows, wide), 1) == iota((rows, wide), 0) + (t * rows).astype(F32)
    owner = jnp.sum(jnp.where(mine, doc_owner[...].astype(F32), 0.0), axis=1, keepdims=True)
    local = jnp.sum(jnp.where(mine, doc_local[...].reshape(1, wide).astype(F32), 0.0), axis=1, keepdims=True)
    step = owner - p.astype(F32)
    step = jnp.where(step < 0.0, step + float(z.n_dp), step)
    step_row = to_row(step, rows)
    same = step == step_row
    above = iota((rows, rows), 0)
    across = iota((rows, rows), 1)
    rank = jnp.sum(jnp.where(same & (across < above), 1.0, 0.0), axis=1, keepdims=True)
    rank_row = jnp.sum(jnp.where(same & (above < across), 1.0, 0.0), axis=0, keepdims=True)
    place = jnp.where(
        rank < float(z.whole),
        step * float(z.whole) + rank,
        float(z.n_dp * z.whole) + step * float(z.rest) + rank - float(z.whole),
    )
    placed = iota((rows, z.lanes), 1) == place
    step_hot = jnp.where(iota((z.n_dp, rows), 0) == step_row, 1.0, 0.0).astype(BF16)
    tags = jnp.dot(
        step_hot,
        jnp.where(placed, local + 1.0, 0.0).astype(BF16),
        preferred_element_type=F32,
    )
    for k in range(z.n_dp):
        tags_out[k] = tags[k : k + 1, :]
    tags_copy = [
        remote(
            tags_out.at[k], tags_in.at[k], tags_send.at[k], tags_recv.at[k],
            dp=lax.rem(p + k, z.n_dp),
        )
        for k in range(1, z.n_dp)
    ]

    member_tag[0] = jnp.where(
        member_valid[...] == 1, member_cluster[...].astype(F32) + 1.0, -1.0
    )
    load_members.wait()
    values = raw[...].astype(F32)
    unit[:, 0] = (
        (values / jnp.sqrt(jnp.sum(values * values, axis=1, keepdims=True) + EPSILON))
        .astype(BF16)
        .reshape(2, z.members // 2, z.emb)
    )
    mtag_copy = [
        remote(
            member_tag.at[0], member_tag.at[j], mtag_send.at[j], mtag_recv.at[j],
            tensor=forward_of(j),
        )
        for j in range(1, z.n_tensor)
    ]

    def head(first, last):
        count = last - first
        total = jnp.dot(
            feat[0, first:last].reshape(count * z.rows, half),
            w1[:half, :],
            preferred_element_type=F32,
        )
        total += jnp.dot(
            feat[1, first:last].reshape(count * z.rows, half),
            w1[half:, :],
            preferred_element_type=F32,
        )
        return jax.nn.gelu(total).astype(BF16)

    def embed(hidden, c, first, last):
        sums_out[c, first:last] = (
            jnp.dot(hidden, w2[:, c * z.cols : (c + 1) * z.cols], preferred_element_type=F32)
            .astype(BF16)
            .reshape(last - first, z.rows, z.cols)
        )

    def send_sums(c, first, last):
        for j in range(first, last):
            sums_copy[c, j] = remote(
                sums_out.at[c, j], sums_in.at[c, j], sums_send.at[c, j], sums_recv.at[c, j],
                tensor=source_of(j),
            )

    sums_copy = {}
    send_own_features(1)
    for j in along_x:
        feat_copy[0, j].wait_recv()
        for y in along_y:
            send_feature(0, corner(j, y), feat.at[0, j], y)
    for j in along_y:
        feat_copy[1, j].wait_recv()
        for x in along_x:
            send_feature(1, corner(x, j), feat.at[1, j], x)
    for copy in (*own, *load_w1, load_w2):
        copy.wait()
    hidden = head(0, 1)
    for c in range(CHUNKS):
        embed(hidden, c, 0, 1)

    near = 1 + len(along_x) + len(along_y)
    for j in along_x:
        feat_copy[1, j].wait_recv()
    for j in along_y:
        feat_copy[0, j].wait_recv()
    if near > 1:
        hidden = head(1, near)
        for c in range(CHUNKS):
            embed(hidden, c, 1, near)
    for j in far:
        feat_copy[0, j].wait_recv()
        feat_copy[1, j].wait_recv()
    send_sums(0, 1, near)
    if far:
        hidden = head(near, z.n_tensor)
    for c in range(CHUNKS):
        if c:
            send_sums(c, 1, near)
        if far:
            embed(hidden, c, near, z.n_tensor)
            send_sums(c, near, z.n_tensor)

    unit_copy = {}

    def send_unit(h, j, held, target):
        unit_copy[h, j] = remote(
            unit.at[h, held], unit.at[h, j], unit_send.at[h, j], unit_recv.at[h, j],
            tensor=forward_of(target),
        )

    code = step_row * float(z.cap) + rank_row
    code = code.reshape(1, 1, rows)
    if z.whole:
        shape = (z.n_dp, z.whole, rows)
        pack_whole = jnp.where(
            code == iota(shape, 0) * float(z.cap) + iota(shape, 1), 1.0, 0.0
        ).reshape(z.n_dp * z.whole, rows).astype(BF16)
    pack_rest = []
    if z.rest:
        shape = (z.n_dp, z.folded, rows)
        for c in range(z.tiles):
            at = iota(shape, 1) - float(c * z.rest)
            inside = (at >= 0.0) & (at < float(z.rest))
            hit = inside & (code == iota(shape, 0) * float(z.cap) + float(z.whole) + at)
            pack_rest.append(
                jnp.where(hit, 1.0, 0.0).reshape(z.n_dp * z.folded, rows).astype(BF16)
            )

    def send_own_units(first):
        for j in along_x:
            send_unit(first, j, 0, j)
        for j in along_y:
            send_unit(1 - first, j, 0, j)

    square = jnp.zeros((rows, 1), F32)
    docs_copy = {}
    for c in range(CHUNKS):
        proj = sums_out[c, 0].astype(F32)
        for j in range(1, z.n_tensor):
            sums_copy[c, j].wait_recv()
            proj += sums_in[c, j].astype(F32)
        query = proj.astype(BF16)
        if z.whole:
            packed = jnp.dot(pack_whole, query, preferred_element_type=F32).astype(BF16)
        if z.rest:
            tail = jnp.zeros((z.n_dp * z.folded, 128), F32)
            for i in range(z.tiles):
                tail += jnp.dot(
                    pack_rest[i], query[:, i * 128 : (i + 1) * 128], preferred_element_type=F32
                )
            tail = tail.astype(BF16)
        for k in [*range(1, z.n_dp), 0]:
            target = docs_out if k else docs_in
            if z.whole:
                for i in range(z.tiles):
                    target[c, k, i * z.whole : (i + 1) * z.whole, :] = packed[
                        k * z.whole : (k + 1) * z.whole, i * 128 : (i + 1) * 128
                    ]
            if z.rest:
                target[c, k, z.tiles * z.whole :, :] = tail[k * z.folded : (k + 1) * z.folded, :]
            if k:
                docs_copy[c, k] = remote(
                    docs_out.at[c, k], docs_in.at[c, k], docs_send.at[c, k], docs_recv.at[c, k],
                    dp=lax.rem(p + k, z.n_dp),
                )
        square += jnp.sum(proj * proj, axis=1, keepdims=True)
        if c == 0:
            send_own_units(0)
    send_own_units(1)
    inverse = 1.0 / jnp.sqrt(square + EPSILON)
    for j in along_x:
        unit_copy[0, j].wait_recv()
        for y in along_y:
            send_unit(0, corner(j, y), j, y)
    for j in along_y:
        unit_copy[1, j].wait_recv()
        for x in along_x:
            send_unit(1, corner(x, j), j, x)

    tag_row = tags_out[0]
    for k in range(1, z.n_dp):
        tags_copy[k - 1].wait_recv()
        tag_row += tags_in[k]
    tag_row = tag_row[:, : z.slots]
    for copy in mtag_copy:
        copy.wait_recv()
    allowed = [to_column(member_tag[j], z.members) for j in range(z.n_tensor)]

    unfold = []
    if z.rest:
        shape = (z.n_dp * z.rest, z.n_dp * z.folded)
        out_row, in_row = iota(shape, 0), iota(shape, 1)
        for i in range(z.tiles):
            hit = jnp.zeros(shape, F32)
            for k in range(z.n_dp):
                at = out_row - float(k * z.rest)
                inside = (at >= 0.0) & (at < float(z.rest))
                hit = jnp.where(
                    inside & (in_row == at + float(k * z.folded + i * z.rest)), 1.0, hit
                )
            unfold.append(hit.astype(BF16))

    arrived = []
    for c in range(CHUNKS):
        for k in range(1, z.n_dp):
            docs_copy[c, k].wait_recv()
        parts = []
        if z.whole:
            parts.append(
                jnp.concatenate(
                    [
                        docs_in[c, :, i * z.whole : (i + 1) * z.whole, :].reshape(
                            z.n_dp * z.whole, 128
                        )
                        for i in range(z.tiles)
                    ],
                    axis=1,
                )
            )
        if z.rest:
            tail = docs_in[c, :, z.tiles * z.whole :, :].reshape(z.n_dp * z.folded, 128)
            parts.append(
                jnp.concatenate(
                    [
                        jnp.dot(unfold[i], tail, preferred_element_type=F32).astype(BF16)
                        for i in range(z.tiles)
                    ],
                    axis=1,
                )
            )
        arrived.append(jnp.concatenate(parts, axis=0) if len(parts) > 1 else parts[0])
    arrived = jnp.concatenate(arrived, axis=1)

    def best_of(first, last):
        scores = lax.dot_general(
            jnp.concatenate(
                [unit[h, j] for j in range(first, last) for h in (0, 1)], axis=0
            ),
            arrived,
            (((1,), (1,)), ((), ())),
            preferred_element_type=F32,
        )
        tags_here = jnp.concatenate(allowed[first:last], axis=0)
        kept = jnp.where(tags_here == tag_row, scores, LOWEST)
        return jnp.max(kept, axis=0, keepdims=True)

    for j in along_x:
        unit_copy[1, j].wait_recv()
    for j in along_y:
        unit_copy[0, j].wait_recv()
    top = best_of(0, near)
    if far:
        for j in far:
            unit_copy[0, j].wait_recv()
            unit_copy[1, j].wait_recv()
        top = jnp.maximum(top, best_of(near, z.n_tensor))
    answer_out[...] = jnp.zeros_like(answer_out)
    answer_out[:, : z.slots] = top

    earlier = list(sent)
    answer_copy = [
        remote(
            answer_out, answer_in.at[k], answer_send.at[k], answer_recv.at[k],
            dp=lax.rem(p + z.n_dp - k, z.n_dp),
        )
        for k in range(1, z.n_dp)
    ]
    for copy in earlier:
        copy.wait_send()
    found = jnp.where(step == 0.0, answer_out[...], 0.0)
    for k in range(1, z.n_dp):
        answer_copy[k - 1].wait_recv()
        found = jnp.where(step == float(k), answer_in[k], found)
    value = jnp.sum(jnp.where(placed, found, 0.0), axis=1, keepdims=True)
    best[...] = to_row(jnp.maximum(value * inverse, -1.0), rows)
    for copy in answer_copy:
        copy.wait_send()


def body(features, w_hidden, w_embed, members, doc_owner, doc_local, member_cluster, member_valid):
    n_dp, n_tensor = lax.axis_size("dp"), lax.axis_size("tensor")
    rows, hid = features.shape
    width, emb = w_embed.shape
    z = Sizes(n_dp, n_tensor, rows, hid, width, emb, members.shape[1])
    half = hid // 2
    dma = pltpu.SemaphoreType.DMA
    hbm = pl.BlockSpec(memory_space=pl.ANY)
    vmem = pl.BlockSpec(memory_space=pltpu.VMEM)
    out = pl.pallas_call(
        functools.partial(kernel, z),
        out_shape=pltpu.VMEM((1, rows), F32),
        in_specs=[hbm] * 8,
        out_specs=vmem,
        scratch_shapes=[
            pltpu.VMEM((2, n_tensor, rows, half), BF16),
            pltpu.VMEM((hid, width), BF16),
            pltpu.VMEM((width, emb), BF16),
            pltpu.VMEM((z.members, emb), BF16),
            pltpu.VMEM((1, doc_owner.shape[0]), jnp.int32),
            pltpu.VMEM(doc_local.shape, jnp.int32),
            pltpu.VMEM((1, z.members), jnp.int32),
            pltpu.VMEM((1, z.members), jnp.int32),
            pltpu.VMEM((2, n_tensor, z.members // 2, emb), BF16),
            pltpu.VMEM((n_tensor, 1, z.members), F32),
            pltpu.VMEM((CHUNKS, n_tensor, rows, z.cols), BF16),
            pltpu.VMEM((CHUNKS, n_tensor, rows, z.cols), BF16),
            pltpu.VMEM((CHUNKS, n_dp, z.block, 128), BF16),
            pltpu.VMEM((CHUNKS, n_dp, z.block, 128), BF16),
            pltpu.VMEM((n_dp, 1, z.lanes), F32),
            pltpu.VMEM((n_dp, 1, z.lanes), F32),
            pltpu.VMEM((1, z.lanes), F32),
            pltpu.VMEM((n_dp, 1, z.lanes), F32),
            dma((10,)),
            dma((2, n_tensor)),
            dma((2, n_tensor)),
            dma((2, n_tensor)),
            dma((2, n_tensor)),
            dma((n_tensor,)),
            dma((n_tensor,)),
            dma((CHUNKS, n_tensor)),
            dma((CHUNKS, n_tensor)),
            dma((CHUNKS, n_dp)),
            dma((CHUNKS, n_dp)),
            dma((n_dp,)),
            dma((n_dp,)),
            dma((n_dp,)),
            dma((n_dp,)),
        ],
        compiler_params=pltpu.CompilerParams(
            collective_id=0, has_side_effects=True, vmem_limit_bytes=62 * 1024 * 1024
        ),
        name="match",
    )(
        features,
        w_hidden,
        w_embed,
        members,
        doc_owner.reshape(1, -1),
        doc_local,
        member_cluster,
        member_valid,
    )
    return out.reshape(rows)


def solution(mesh):
    return jax.shard_map(
        body,
        mesh=mesh,
        in_specs=(
            P(("dp", "tensor"), None),
            P(None, "tensor"),
            P("tensor", None),
            P("dp", "tensor", None),
            P("dp", None),
            P("dp"),
            P("dp", "tensor"),
            P("dp", "tensor"),
        ),
        out_specs=P(("dp", "tensor")),
        check_vma=False,
    )
```

```python
import functools
import math

import jax
import jax.numpy as jnp
from jax import lax
from jax.experimental import pallas as pl
from jax.experimental.pallas import tpu as pltpu
from jax.sharding import PartitionSpec as P

EPSILON = 1e-06
MESH = pl.DeviceIdType.MESH
F32 = jnp.float32
BF16 = jnp.bfloat16
LOWEST = -1e30
CHUNKS = 2


def iota(shape, dim):
    return lax.broadcasted_iota(jnp.int32, shape, dim).astype(F32)


def to_column(row, size):
    eye = iota((size, size), 0) == iota((size, size), 1)
    return jnp.sum(jnp.where(eye, row, 0.0), axis=1, keepdims=True)


def to_row(column, size):
    eye = iota((size, size), 0) == iota((size, size), 1)
    return jnp.sum(jnp.where(eye, column, 0.0), axis=0, keepdims=True)


class Sizes:
    def __init__(self, n_dp, n_tensor, rows, hid, width, emb, members):
        self.n_dp, self.n_tensor = n_dp, n_tensor
        self.rows, self.hid, self.width, self.emb, self.members = rows, hid, width, emb, members
        self.nx = max(d for d in range(1, math.isqrt(n_tensor) + 1) if n_tensor % d == 0)
        self.ny = n_tensor // self.nx
        shifts = [(x, y) for y in range(self.ny) for x in range(self.nx)]
        self.shifts = sorted(shifts, key=lambda xy: ((xy[0] > 0) + (xy[1] > 0), xy[1], xy[0]))
        self.along_x = [j for j, (x, y) in enumerate(self.shifts) if x and not y]
        self.along_y = [j for j, (x, y) in enumerate(self.shifts) if y and not x]
        self.far = [j for j, (x, y) in enumerate(self.shifts) if x and y]
        self.cap = min(rows, max(2, 2 * rows // n_dp))
        self.whole = self.cap // 16 * 16
        self.rest = self.cap - self.whole
        self.cols = emb // CHUNKS
        self.tiles = self.cols // 128
        self.folded = -(-self.rest * self.tiles // 16) * 16
        self.block = self.whole * self.tiles + self.folded
        self.slots = n_dp * self.cap
        self.lanes = -(-self.slots // 128) * 128


def kernel(
    z,
    features,
    w_hidden,
    w_embed,
    members,
    hbm_owner,
    hbm_local,
    hbm_cluster,
    hbm_valid,
    best,
    feat,
    w1,
    w2,
    raw,
    doc_owner,
    doc_local,
    member_cluster,
    member_valid,
    unit,
    member_tag,
    sums_out,
    sums_in,
    docs_out,
    docs_in,
    tags_out,
    tags_in,
    answer_out,
    answer_in,
    local_sem,
    feat_send,
    feat_recv,
    unit_send,
    unit_recv,
    mtag_send,
    mtag_recv,
    sums_send,
    sums_recv,
    docs_send,
    docs_recv,
    tags_send,
    tags_recv,
    answer_send,
    answer_recv,
):
    p = lax.axis_index("dp")
    t = lax.axis_index("tensor")
    tx, ty = lax.rem(t, z.nx), lax.div(t, z.nx)
    half = z.hid // 2
    sent = []

    def forward_of(j):
        dx, dy = z.shifts[j]
        return lax.rem(ty + dy, z.ny) * z.nx + lax.rem(tx + dx, z.nx)

    def source_of(j):
        dx, dy = z.shifts[j]
        return lax.rem(ty + z.ny - dy, z.ny) * z.nx + lax.rem(tx + z.nx - dx, z.nx)

    def remote(src, dst, send, recv, **device):
        copy = pltpu.make_async_remote_copy(
            src_ref=src, dst_ref=dst, send_sem=send, recv_sem=recv, device_id=device,
            device_id_type=MESH,
        )
        copy.start()
        sent.append(copy)
        return copy

    barrier = pltpu.get_barrier_semaphore()
    for j in range(1, z.n_tensor):
        pl.semaphore_signal(barrier, inc=1, device_id={"tensor": forward_of(j)}, device_id_type=MESH)
    for k in range(1, z.n_dp):
        pl.semaphore_signal(
            barrier, inc=1, device_id={"dp": lax.rem(p + k, z.n_dp)}, device_id_type=MESH
        )

    own = [
        pltpu.make_async_copy(features.at[:, pl.ds(h * half, half)], feat.at[h, 0], local_sem.at[h])
        for h in (0, 1)
    ]
    load_w1 = [
        pltpu.make_async_copy(
            w_hidden.at[pl.ds(h * half, half)], w1.at[pl.ds(h * half, half)], local_sem.at[2 + h]
        )
        for h in (0, 1)
    ]
    load_w2 = pltpu.make_async_copy(w_embed, w2, local_sem.at[4])
    load_members = pltpu.make_async_copy(members.at[0], raw, local_sem.at[5])
    load_small = [
        pltpu.make_async_copy(src, dst, local_sem.at[6 + i])
        for i, (src, dst) in enumerate(
            (
                (hbm_owner, doc_owner),
                (hbm_local, doc_local),
                (hbm_cluster, member_cluster),
                (hbm_valid, member_valid),
            )
        )
    ]
    for copy in (*load_small, *own, *load_w1, load_w2, load_members):
        copy.start()

    pl.semaphore_wait(barrier, z.n_tensor - 1 + z.n_dp - 1)

    feat_copy = {}

    def send_feature(h, j, src, target):
        feat_copy[h, j] = remote(
            src, feat.at[h, j], feat_send.at[h, j], feat_recv.at[h, j], tensor=forward_of(target)
        )

    along_x, along_y, far = z.along_x, z.along_y, z.far

    def corner(x, y):
        return z.shifts.index((z.shifts[x][0], z.shifts[y][1]))

    def send_own_features(first):
        for j in along_x:
            send_feature(first, j, features.at[:, pl.ds(first * half, half)], j)
        for j in along_y:
            send_feature(1 - first, j, features.at[:, pl.ds((1 - first) * half, half)], j)

    send_own_features(0)

    for copy in load_small:
        copy.wait()
    rows, wide = z.rows, doc_owner.shape[1]
    mine = iota((rows, wide), 1) == iota((rows, wide), 0) + (t * rows).astype(F32)
    owner = jnp.sum(jnp.where(mine, doc_owner[...].astype(F32), 0.0), axis=1, keepdims=True)
    local = jnp.sum(jnp.where(mine, doc_local[...].reshape(1, wide).astype(F32), 0.0), axis=1, keepdims=True)
    step = owner - p.astype(F32)
    step = jnp.where(step < 0.0, step + float(z.n_dp), step)
    step_row = to_row(step, rows)
    same = step == step_row
    above = iota((rows, rows), 0)
    across = iota((rows, rows), 1)
    rank = jnp.sum(jnp.where(same & (across < above), 1.0, 0.0), axis=1, keepdims=True)
    rank_row = jnp.sum(jnp.where(same & (above < across), 1.0, 0.0), axis=0, keepdims=True)
    place = jnp.where(
        rank < float(z.whole),
        step * float(z.whole) + rank,
        float(z.n_dp * z.whole) + step * float(z.rest) + rank - float(z.whole),
    )
    placed = iota((rows, z.lanes), 1) == place
    step_hot = jnp.where(iota((z.n_dp, rows), 0) == step_row, 1.0, 0.0).astype(BF16)
    tags = jnp.dot(
        step_hot,
        jnp.where(placed, local + 1.0, 0.0).astype(BF16),
        preferred_element_type=F32,
    )
    for k in range(z.n_dp):
        tags_out[k] = tags[k : k + 1, :]
    tags_copy = [
        remote(
            tags_out.at[k], tags_in.at[k], tags_send.at[k], tags_recv.at[k],
            dp=lax.rem(p + k, z.n_dp),
        )
        for k in range(1, z.n_dp)
    ]

    member_tag[0] = jnp.where(
        member_valid[...] == 1, member_cluster[...].astype(F32) + 1.0, -1.0
    )
    load_members.wait()
    values = raw[...].astype(F32)
    unit[:, 0] = (
        (values / jnp.sqrt(jnp.sum(values * values, axis=1, keepdims=True) + EPSILON))
        .astype(BF16)
        .reshape(2, z.members // 2, z.emb)
    )
    mtag_copy = [
        remote(
            member_tag.at[0], member_tag.at[j], mtag_send.at[j], mtag_recv.at[j],
            tensor=forward_of(j),
        )
        for j in range(1, z.n_tensor)
    ]

    def head(first, last):
        count = last - first
        total = jnp.dot(
            feat[0, first:last].reshape(count * z.rows, half),
            w1[:half, :],
            preferred_element_type=F32,
        )
        total += jnp.dot(
            feat[1, first:last].reshape(count * z.rows, half),
            w1[half:, :],
            preferred_element_type=F32,
        )
        return jax.nn.gelu(total).astype(BF16)

    def embed(hidden, c, first, last):
        sums_out[c, first:last] = (
            jnp.dot(hidden, w2[:, c * z.cols : (c + 1) * z.cols], preferred_element_type=F32)
            .astype(BF16)
            .reshape(last - first, z.rows, z.cols)
        )

    def send_sums(c, first, last):
        for j in range(first, last):
            sums_copy[c, j] = remote(
                sums_out.at[c, j], sums_in.at[c, j], sums_send.at[c, j], sums_recv.at[c, j],
                tensor=source_of(j),
            )

    sums_copy = {}
    send_own_features(1)
    for j in along_x:
        feat_copy[0, j].wait_recv()
        for y in along_y:
            send_feature(0, corner(j, y), feat.at[0, j], y)
    for j in along_y:
        feat_copy[1, j].wait_recv()
        for x in along_x:
            send_feature(1, corner(x, j), feat.at[1, j], x)
    for copy in (*own, *load_w1, load_w2):
        copy.wait()
    hidden = head(0, 1)
    for c in range(CHUNKS):
        embed(hidden, c, 0, 1)

    near = 1 + len(along_x) + len(along_y)
    for j in along_x:
        feat_copy[1, j].wait_recv()
    for j in along_y:
        feat_copy[0, j].wait_recv()
    if near > 1:
        hidden = head(1, near)
        for c in range(CHUNKS):
            embed(hidden, c, 1, near)
    for j in far:
        feat_copy[0, j].wait_recv()
        feat_copy[1, j].wait_recv()
    send_sums(0, 1, near)
    if far:
        hidden = head(near, z.n_tensor)
    for c in range(CHUNKS):
        if c:
            send_sums(c, 1, near)
        if far:
            embed(hidden, c, near, z.n_tensor)
            send_sums(c, near, z.n_tensor)

    unit_copy = {}

    def send_unit(h, j, held, target):
        unit_copy[h, j] = remote(
            unit.at[h, held], unit.at[h, j], unit_send.at[h, j], unit_recv.at[h, j],
            tensor=forward_of(target),
        )

    def send_own_units(first):
        for j in along_x:
            send_unit(first, j, 0, j)
        for j in along_y:
            send_unit(1 - first, j, 0, j)

    send_own_units(0)

    code = step_row * float(z.cap) + rank_row
    code = code.reshape(1, 1, rows)
    if z.whole:
        shape = (z.n_dp, z.whole, rows)
        pack_whole = jnp.where(
            code == iota(shape, 0) * float(z.cap) + iota(shape, 1), 1.0, 0.0
        ).reshape(z.n_dp * z.whole, rows).astype(BF16)
    pack_rest = []
    if z.rest:
        shape = (z.n_dp, z.folded, rows)
        for c in range(z.tiles):
            at = iota(shape, 1) - float(c * z.rest)
            inside = (at >= 0.0) & (at < float(z.rest))
            hit = inside & (code == iota(shape, 0) * float(z.cap) + float(z.whole) + at)
            pack_rest.append(
                jnp.where(hit, 1.0, 0.0).reshape(z.n_dp * z.folded, rows).astype(BF16)
            )

    square = jnp.zeros((rows, 1), F32)
    docs_copy = {}
    for c in range(CHUNKS):
        proj = sums_out[c, 0].astype(F32)
        for j in range(1, z.n_tensor):
            sums_copy[c, j].wait_recv()
            proj += sums_in[c, j].astype(F32)
        query = proj.astype(BF16)
        if z.whole:
            packed = jnp.dot(pack_whole, query, preferred_element_type=F32).astype(BF16)
        if z.rest:
            tail = jnp.zeros((z.n_dp * z.folded, 128), F32)
            for i in range(z.tiles):
                tail += jnp.dot(
                    pack_rest[i], query[:, i * 128 : (i + 1) * 128], preferred_element_type=F32
                )
            tail = tail.astype(BF16)
        for k in [*range(1, z.n_dp), 0]:
            target = docs_out if k else docs_in
            if z.whole:
                for i in range(z.tiles):
                    target[c, k, i * z.whole : (i + 1) * z.whole, :] = packed[
                        k * z.whole : (k + 1) * z.whole, i * 128 : (i + 1) * 128
                    ]
            if z.rest:
                target[c, k, z.tiles * z.whole :, :] = tail[k * z.folded : (k + 1) * z.folded, :]
            if k:
                docs_copy[c, k] = remote(
                    docs_out.at[c, k], docs_in.at[c, k], docs_send.at[c, k], docs_recv.at[c, k],
                    dp=lax.rem(p + k, z.n_dp),
                )
        square += jnp.sum(proj * proj, axis=1, keepdims=True)
        if c == 0:
            send_own_units(1)
    inverse = 1.0 / jnp.sqrt(square + EPSILON)
    for j in along_x:
        unit_copy[0, j].wait_recv()
        for y in along_y:
            send_unit(0, corner(j, y), j, y)
    for j in along_y:
        unit_copy[1, j].wait_recv()
        for x in along_x:
            send_unit(1, corner(x, j), j, x)

    tag_row = tags_out[0]
    for k in range(1, z.n_dp):
        tags_copy[k - 1].wait_recv()
        tag_row += tags_in[k]
    tag_row = tag_row[:, : z.slots]
    for copy in mtag_copy:
        copy.wait_recv()
    allowed = [to_column(member_tag[j], z.members) for j in range(z.n_tensor)]

    unfold = []
    if z.rest:
        shape = (z.n_dp * z.rest, z.n_dp * z.folded)
        out_row, in_row = iota(shape, 0), iota(shape, 1)
        for i in range(z.tiles):
            hit = jnp.zeros(shape, F32)
            for k in range(z.n_dp):
                at = out_row - float(k * z.rest)
                inside = (at >= 0.0) & (at < float(z.rest))
                hit = jnp.where(
                    inside & (in_row == at + float(k * z.folded + i * z.rest)), 1.0, hit
                )
            unfold.append(hit.astype(BF16))

    arrived = []
    for c in range(CHUNKS):
        for k in range(1, z.n_dp):
            docs_copy[c, k].wait_recv()
        parts = []
        if z.whole:
            parts.append(
                jnp.concatenate(
                    [
                        docs_in[c, :, i * z.whole : (i + 1) * z.whole, :].reshape(
                            z.n_dp * z.whole, 128
                        )
                        for i in range(z.tiles)
                    ],
                    axis=1,
                )
            )
        if z.rest:
            tail = docs_in[c, :, z.tiles * z.whole :, :].reshape(z.n_dp * z.folded, 128)
            parts.append(
                jnp.concatenate(
                    [
                        jnp.dot(unfold[i], tail, preferred_element_type=F32).astype(BF16)
                        for i in range(z.tiles)
                    ],
                    axis=1,
                )
            )
        arrived.append(jnp.concatenate(parts, axis=0) if len(parts) > 1 else parts[0])
    arrived = jnp.concatenate(arrived, axis=1)

    def best_of(first, last):
        scores = lax.dot_general(
            jnp.concatenate(
                [unit[h, j] for j in range(first, last) for h in (0, 1)], axis=0
            ),
            arrived,
            (((1,), (1,)), ((), ())),
            preferred_element_type=F32,
        )
        tags_here = jnp.concatenate(allowed[first:last], axis=0)
        kept = jnp.where(tags_here == tag_row, scores, LOWEST)
        return jnp.max(kept, axis=0, keepdims=True)

    for j in along_x:
        unit_copy[1, j].wait_recv()
    for j in along_y:
        unit_copy[0, j].wait_recv()
    top = best_of(0, near)
    if far:
        for j in far:
            unit_copy[0, j].wait_recv()
            unit_copy[1, j].wait_recv()
        top = jnp.maximum(top, best_of(near, z.n_tensor))
    answer_out[...] = jnp.zeros_like(answer_out)
    answer_out[:, : z.slots] = top

    earlier = list(sent)
    answer_copy = [
        remote(
            answer_out, answer_in.at[k], answer_send.at[k], answer_recv.at[k],
            dp=lax.rem(p + z.n_dp - k, z.n_dp),
        )
        for k in range(1, z.n_dp)
    ]
    for copy in earlier:
        copy.wait_send()
    found = jnp.where(step == 0.0, answer_out[...], 0.0)
    for k in range(1, z.n_dp):
        answer_copy[k - 1].wait_recv()
        found = jnp.where(step == float(k), answer_in[k], found)
    value = jnp.sum(jnp.where(placed, found, 0.0), axis=1, keepdims=True)
    best[...] = to_row(jnp.maximum(value * inverse, -1.0), rows)
    for copy in answer_copy:
        copy.wait_send()


def body(features, w_hidden, w_embed, members, doc_owner, doc_local, member_cluster, member_valid):
    n_dp, n_tensor = lax.axis_size("dp"), lax.axis_size("tensor")
    rows, hid = features.shape
    width, emb = w_embed.shape
    z = Sizes(n_dp, n_tensor, rows, hid, width, emb, members.shape[1])
    half = hid // 2
    dma = pltpu.SemaphoreType.DMA
    hbm = pl.BlockSpec(memory_space=pl.ANY)
    vmem = pl.BlockSpec(memory_space=pltpu.VMEM)
    out = pl.pallas_call(
        functools.partial(kernel, z),
        out_shape=pltpu.VMEM((1, rows), F32),
        in_specs=[hbm] * 8,
        out_specs=vmem,
        scratch_shapes=[
            pltpu.VMEM((2, n_tensor, rows, half), BF16),
            pltpu.VMEM((hid, width), BF16),
            pltpu.VMEM((width, emb), BF16),
            pltpu.VMEM((z.members, emb), BF16),
            pltpu.VMEM((1, doc_owner.shape[0]), jnp.int32),
            pltpu.VMEM(doc_local.shape, jnp.int32),
            pltpu.VMEM((1, z.members), jnp.int32),
            pltpu.VMEM((1, z.members), jnp.int32),
            pltpu.VMEM((2, n_tensor, z.members // 2, emb), BF16),
            pltpu.VMEM((n_tensor, 1, z.members), F32),
            pltpu.VMEM((CHUNKS, n_tensor, rows, z.cols), BF16),
            pltpu.VMEM((CHUNKS, n_tensor, rows, z.cols), BF16),
            pltpu.VMEM((CHUNKS, n_dp, z.block, 128), BF16),
            pltpu.VMEM((CHUNKS, n_dp, z.block, 128), BF16),
            pltpu.VMEM((n_dp, 1, z.lanes), F32),
            pltpu.VMEM((n_dp, 1, z.lanes), F32),
            pltpu.VMEM((1, z.lanes), F32),
            pltpu.VMEM((n_dp, 1, z.lanes), F32),
            dma((10,)),
            dma((2, n_tensor)),
            dma((2, n_tensor)),
            dma((2, n_tensor)),
            dma((2, n_tensor)),
            dma((n_tensor,)),
            dma((n_tensor,)),
            dma((CHUNKS, n_tensor)),
            dma((CHUNKS, n_tensor)),
            dma((CHUNKS, n_dp)),
            dma((CHUNKS, n_dp)),
            dma((n_dp,)),
            dma((n_dp,)),
            dma((n_dp,)),
            dma((n_dp,)),
        ],
        compiler_params=pltpu.CompilerParams(
            collective_id=0, has_side_effects=True, vmem_limit_bytes=62 * 1024 * 1024
        ),
        name="match",
    )(
        features,
        w_hidden,
        w_embed,
        members,
        doc_owner.reshape(1, -1),
        doc_local,
        member_cluster,
        member_valid,
    )
    return out.reshape(rows)


def solution(mesh):
    return jax.shard_map(
        body,
        mesh=mesh,
        in_specs=(
            P(("dp", "tensor"), None),
            P(None, "tensor"),
            P("tensor", None),
            P("dp", "tensor", None),
            P("dp", None),
            P("dp"),
            P("dp", "tensor"),
            P("dp", "tensor"),
        ),
        out_specs=P(("dp", "tensor")),
        check_vma=False,
    )
```
